256 devices in a mesh: phase: 4 (over z_hi, core), slab: 64 (over y, x, z_lo).
Axes of the slice: x: 4, y: 4, z: 8 (z_hi: 2, z_lo: 4; z = z_hi * 4 + z_lo), core: 2. Of those that a mesh axis runs over, the one named last changes fastest.
Arguments:
- template: bfloat16 [64, 384, 384], P('slab'), may hold values from -6 to 6
- phase_images: bfloat16 [4, 64, 384, 384], P('phase', 'slab'), may hold values from -6 to 6
- corner: int32 [4, 64, 384, 384], P('phase', 'slab'), may hold values from 0 to 7, as said below
- fractions: bfloat16 [4, 3, 64, 384, 384], P('phase', None, 'slab'), may hold values from 0 to 1
- start_modes: float32 [4, 6, 4096], P('phase', None, 'slab'), may hold values from -6 to 6
Outputs:
- centred_modes: float32 [4, 6, 4096], P('phase', None, 'slab')
- velocity: bfloat16 [4, 3, 64, 384, 384], P('phase', None, 'slab')
The draws below stay inside these ranges and needn't reach their ends.
Inputs may be any that keep to these rules, and one draw needn't show every extreme that they name: `corner`: each phase's first voxel has code 0 and its last voxel code 7.
All inputs are finite; a program needn't handle non-finite values.
Results may differ from the reference program's by a relative error of at most 0.0055.
Values may be sent and summed in bfloat16 or wider, within the bound.
A program may use at most 64 MiB of HBM per device.

```python
import math
import jax
import jax.numpy as jnp
from jax import lax

NX = 384
NY = 384
KM = 16
STEPS = 2
NPH = 4
NZ = 64
MODES = 4096


def draw_corner(key, part):
    key = jax.random.fold_in(key, 11)
    shape = (NPH, NZ, NY, NX)
    code = jax.random.randint(key, shape, 0, 8)
    plane = lax.broadcasted_iota(jnp.int32, shape, 1)
    row = lax.broadcasted_iota(jnp.int32, shape, 2)
    col = lax.broadcasted_iota(jnp.int32, shape, 3)
    first = (plane == 0) & (row == 0) & (col == 0)
    final = (plane == NZ - 1) & (row == NY - 1) & (col == NX - 1)
    code = jnp.where(first, 0, jnp.where(final, 7, code))
    return code.astype(jnp.int32)


def shard_levels(stream_key, dims, pieces, least, high):
    factor_of, own = 1.0, jax.random.fold_in(stream_key, 6)
    for dim, blocks in pieces:
        draws = jnp.exp(jax.random.uniform(jax.random.fold_in(own, dim), (blocks,), jnp.float32, least / len(pieces), high / len(pieces)))
        factor_of = factor_of * jnp.repeat(draws, dims[dim] // blocks).reshape([-1 if axis == dim else 1 for axis in range(len(dims))])
    return factor_of


def gaussian(stream_key, extent, spread, reach, cuts=(), kind=jnp.bfloat16):
    entries = spread * jax.random.normal(stream_key, extent, jnp.float32)
    if cuts:
        entries = entries * shard_levels(stream_key, extent, cuts, -0.22, 0.18)
    return jnp.clip(entries, -reach, reach).astype(kind)


def setup_inputs(seed: int = 0) -> dict:
    keys = jax.random.split(jax.random.key(seed), 6)
    template = gaussian(keys[0], (NZ, NY, NX), 1.0, 6.0, ((0, 64),))
    phase_images = gaussian(keys[1], (NPH, NZ, NY, NX), 1.0, 6.0, ((0, 4), (1, 64)))
    corner = draw_corner(jax.random.fold_in(keys[5], 71), 0)
    fractions = jnp.clip(1.0 * jax.random.uniform(keys[3], (NPH, 3, NZ, NY, NX), jnp.float32) ** shard_levels(keys[3], (NPH, 3, NZ, NY, NX), ((0, 4), (2, 64)), -0.2, 0.2), 0.0, 1.0).astype(jnp.bfloat16)
    start_modes = gaussian(keys[4], (NPH, 6, MODES), 1.0, 6.0, ((0, 4), (2, 64)), jnp.float32)
    return dict(template=template, phase_images=phase_images, corner=corner, fractions=fractions, start_modes=start_modes)


HIGH = lax.Precision.HIGHEST
step_size = 0.5
alpha_reg = 0.002
time_step = 0.025

def ein(spec, left, right):
    return jnp.einsum(spec, left, right, precision=HIGH, preferred_element_type=jnp.float32)

def wave_table(count, start, length, modes, scale):
    places = start + jnp.arange(count, dtype=jnp.int32)
    freq = jnp.arange(modes, dtype=jnp.int32) - modes // 2
    wrapped = jnp.mod(places[:, None] * freq[None, :], length)
    angle = wrapped.astype(jnp.float32) * (2.0 * math.pi / length)
    return (jnp.cos(angle) * scale, jnp.sin(angle) * scale)

def cpass(spec, real_part, imag_part, cosine, sine, sign):
    rc = ein(spec, real_part, cosine)
    rs = ein(spec, real_part, sine)
    if imag_part is None:
        return (rc, sign * rs)
    ic = ein(spec, imag_part, cosine)
    isn = ein(spec, imag_part, sine)
    if sign > 0:
        return (rc - isn, rs + ic)
    return (rc + isn, ic - rs)

def real_pass(spec, real_part, imag_part, cosine, sine):
    return ein(spec, real_part, cosine) - ein(spec, imag_part, sine)

def shift_axis(array, axis, lead, offset):
    count = array.shape[axis]
    if lead < 0:
        first = lax.slice_in_dim(array, offset, offset + 1, axis=axis)
        rest = lax.slice_in_dim(array, offset, count - 1 + offset, axis=axis)
        return jnp.concatenate([first, rest], axis=axis)
    rest = lax.slice_in_dim(array, offset, count - 1 + offset, axis=axis)
    final = lax.slice_in_dim(array, count - 2 + offset, count - 1 + offset, axis=axis)
    return jnp.concatenate([rest, final], axis=axis)

def warp(padded, code, frac):
    depth = code.shape[0]
    lifted = code // 4 == 1
    same_y = code // 2 % 2 == 1
    same_x = code % 2 == 1
    parts = [frac[0].astype(jnp.float32), frac[1].astype(jnp.float32), frac[2].astype(jnp.float32)]
    total = jnp.zeros(code.shape, jnp.float32)
    for step_z in (0, 1):
        weight_z = parts[0] if step_z else 1.0 - parts[0]
        for step_y in (0, 1):
            weight_y = parts[1] if step_y else 1.0 - parts[1]
            for step_x in (0, 1):
                weight_x = parts[2] if step_x else 1.0 - parts[2]
                picked = []
                for raise_z in (0, 1):
                    plane = lax.slice_in_dim(padded, raise_z + step_z, raise_z + step_z + depth, axis=0)
                    x_low = shift_axis(plane, 2, -1, step_x)
                    x_same = shift_axis(plane, 2, 0, step_x)
                    low_row = jnp.where(same_x, shift_axis(x_same, 1, -1, step_y), shift_axis(x_low, 1, -1, step_y))
                    same_row = jnp.where(same_x, shift_axis(x_same, 1, 0, step_y), shift_axis(x_low, 1, 0, step_y))
                    picked.append(jnp.where(same_y, same_row, low_row))
                sample = jnp.where(lifted, picked[1], picked[0])
                total = total + weight_z * weight_y * weight_x * sample.astype(jnp.float32)
    return total.astype(jnp.bfloat16)

def gradient(rimmed):
    values = rimmed.astype(jnp.float32)
    centre = values[1:-1]
    grad_z = (values[2:] - values[:-2]) * 0.5
    along_y = jnp.pad(centre, ((0, 0), (1, 1), (0, 0)))
    grad_y = (along_y[:, 2:] - along_y[:, :-2]) * 0.5
    along_x = jnp.pad(centre, ((0, 0), (0, 0), (1, 1)))
    grad_x = (along_x[:, :, 2:] - along_x[:, :, :-2]) * 0.5
    return jnp.stack([grad_z, grad_y, grad_x])

def analyse_planes(force, xcos, xsin, ycos, ysin):
    xr, xi = cpass('czyx,xk->czyk', force, None, xcos, xsin, -1)
    return cpass('czyk,yj->czjk', xr, xi, ycos, ysin, -1)

def z_modes(yr, yi, zcos, zsin):
    zr, zi = cpass('czjk,zl->cjkl', yr, yi, zcos, zsin, -1)
    return jnp.concatenate([zr.reshape(3, -1), zi.reshape(3, -1)])

def kernel_at(flat, modes):
    half = modes // 2
    freq_y = flat // (modes * modes) - half
    freq_x = flat // modes % modes - half
    freq_z = flat % modes - half
    squares = (freq_y * freq_y + freq_x * freq_x + freq_z * freq_z).astype(jnp.float32)
    return 1.0 / (1.0 + alpha_reg * squares) ** 2

def synth_grid(real_part, imag_part, zcos, zsin, cosine, sine):
    real_part, imag_part = cpass('nabk,gk->nabg', real_part, imag_part, zcos, zsin, 1)
    real_part, imag_part = cpass('nakc,gk->nagc', real_part, imag_part, cosine, sine, 1)
    return real_pass('nkbc,gk->ngbc', real_part, imag_part, cosine, sine)

def analyse_grid(field, zcos, zsin, cosine, sine):
    real_part, imag_part = cpass('nabg,gk->nabk', field, None, zcos, zsin, -1)
    real_part, imag_part = cpass('nagc,gk->nakc', real_part, imag_part, cosine, sine, -1)
    return cpass('ngbc,gk->nkbc', real_part, imag_part, cosine, sine, -1)

def shoot(modes, size, steps):
    cosine, sine = wave_table(size, 0, size, size, 1.0)
    norm = float(size) ** (-1.5)
    zcos, zsin = (cosine * norm, sine * norm)
    whole = jnp.arange(size, dtype=jnp.int32) - size // 2
    freq = whole.astype(jnp.float32) * (2.0 * math.pi / size)
    waves = [freq[None, None, :], freq[:, None, None], freq[None, :, None]]
    squares = (whole[:, None, None] ** 2 + whole[None, :, None] ** 2 + whole[None, None, :] ** 2).astype(jnp.float32)
    inertia = (1.0 + alpha_reg * squares) ** 2
    kernel = 1.0 / inertia
    vel_re = modes[:3].reshape(3, size, size, size)
    vel_im = modes[3:].reshape(3, size, size, size)
    for step in range(steps):
        mom_re = inertia * vel_re
        mom_im = inertia * vel_im
        deriv_re = jnp.concatenate([-waves[axis] * vel_im for axis in range(3)])
        deriv_im = jnp.concatenate([waves[axis] * vel_re for axis in range(3)])
        fields = synth_grid(jnp.concatenate([vel_re, mom_re, deriv_re]), jnp.concatenate([vel_im, mom_im, deriv_im]), zcos, zsin, cosine, sine)
        speed = fields[:3]
        momentum = fields[3:6]
        deriv = fields[6:].reshape(3, 3, size, size, size)
        advect = lax.optimization_barrier(jnp.sum(deriv * momentum[None], axis=1))
        outer = (momentum[:, None] * speed[None, :]).reshape(9, size, size, size)
        spec_re, spec_im = analyse_grid(jnp.concatenate([advect, outer]), zcos, zsin, cosine, sine)
        outer_re = spec_re[3:].reshape(3, 3, size, size, size)
        outer_im = spec_im[3:].reshape(3, 3, size, size, size)
        coad_re = spec_re[:3] - (waves[0] * outer_im[:, 0] + waves[1] * outer_im[:, 1] + waves[2] * outer_im[:, 2])
        coad_im = spec_im[:3] + (waves[0] * outer_re[:, 0] + waves[1] * outer_re[:, 1] + waves[2] * outer_re[:, 2])
        vel_re = vel_re - time_step * kernel * coad_re
        vel_im = vel_im - time_step * kernel * coad_im
    return jnp.concatenate([vel_re.reshape(3, -1), vel_im.reshape(3, -1)])

def synth_fine(modes, size, zcos, zsin, ycos, ysin, xcos, xsin):
    vel_re = modes[:3].reshape(3, size, size, size)
    vel_im = modes[3:].reshape(3, size, size, size)
    zr, zi = cpass('cjkl,zl->czjk', vel_re, vel_im, zcos, zsin, 1)
    yr, yi = cpass('czjk,yj->czyk', zr, zi, ycos, ysin, 1)
    return real_pass('czyk,xk->czyx', yr, yi, xcos, xsin)

def reference(template, phase_images, corner, fractions, start_modes):
    padded = jnp.pad(template, ((1, 1), (0, 0), (0, 0)))
    xcos, xsin = wave_table(NX, 0, NX, KM, 1.0)
    ycos, ysin = wave_table(NY, 0, NY, KM, 1.0)
    zcos, zsin = wave_table(NZ, 0, NZ, KM, 1.0 / math.sqrt(NX * NY * NZ))
    fine_zcos, fine_zsin = wave_table(NZ, 0, NZ, KM, float(KM) ** (-1.5))

    def per_phase(item):
        image, code, frac = item
        warped = warp(padded, code, frac)
        rimmed = jnp.pad(warped, ((1, 1), (0, 0), (0, 0)))
        force = (image.astype(jnp.float32) - warped.astype(jnp.float32)) * gradient(rimmed)
        yr, yi = analyse_planes(force, xcos, xsin, ycos, ysin)
        return z_modes(yr, yi, zcos, zsin)
    gradient_modes = lax.map(per_phase, (phase_images, corner, fractions))
    flat = jnp.arange(KM * KM * KM, dtype=jnp.int32)
    update = (1.0 - step_size) * start_modes + step_size * kernel_at(flat, KM)[None, None] * gradient_modes
    centred_modes = update - lax.optimization_barrier(jnp.mean(update, axis=0, keepdims=True))

    def per_shot(modes):
        shot = shoot(modes, KM, STEPS)
        return synth_fine(shot, KM, fine_zcos, fine_zsin, ycos, ysin, xcos, xsin).astype(jnp.bfloat16)
    velocity = lax.map(per_shot, centred_modes)
    return (centred_modes, velocity)
```

```python
import functools
import math

import ml_dtypes
import numpy as np

import jax
import jax.numpy as jnp
from jax import lax
from jax.experimental import pallas as pl
from jax.experimental.pallas import tpu as pltpu
from jax.sharding import PartitionSpec as P

KM = 16
STEPS = 2
ZLO = 4
CHUNKS = 4
BLK = 16
HIGH = lax.Precision.HIGHEST
MESH = pl.DeviceIdType.MESH
step_size = 0.5
alpha_reg = 0.002
time_step = 0.025
F32 = jnp.float32
BF16 = jnp.bfloat16
VMEM = pltpu.VMEM


def wave(count, length, modes):
    places = np.arange(count, dtype=np.int64)
    freq = np.arange(modes, dtype=np.int64) - modes // 2
    angle = np.mod(places[:, None] * freq[None, :], length) * (2.0 * math.pi / length)
    return np.cos(angle), np.sin(angle)


def split(table):
    table = np.asarray(table, np.float32)
    high = table.astype(ml_dtypes.bfloat16)
    low = (table - high.astype(np.float32)).astype(ml_dtypes.bfloat16)
    return high, low


def halves(value):
    high = value.astype(BF16)
    low = (value - high.astype(F32)).astype(BF16)
    return high, low


def dot(left, right):
    return jnp.dot(left, right, preferred_element_type=F32)


def analysis_tables(rows, cols):
    ycos, ysin = wave(rows, rows, KM)
    xcos, xsin = wave(cols, cols, KM)
    yt = np.concatenate(split(np.concatenate([ycos.T, -ysin.T])))
    spread = np.concatenate([np.tile(xcos, (1, KM)), np.tile(xsin, (1, KM))], axis=1)
    xt = np.stack(split(spread))
    return yt, xt


def shooting_tables(slabs, rows, cols):
    m = KM
    zcos, zsin = wave(slabs, slabs, m)
    scale = 1.0 / math.sqrt(rows * cols * slabs)
    lift = np.zeros((2, 2, 3, m, slabs, 16))
    for half in range(2):
        for comp in range(3):
            real, imag = comp * 4 + half, comp * 4 + 2 + half
            lift[half, 0, comp, :, :, real] = zcos.T * scale
            lift[half, 0, comp, :, :, imag] = zsin.T * scale
            lift[half, 1, comp, :, :, imag] = zcos.T * scale
            lift[half, 1, comp, :, :, real] = -zsin.T * scale
    lift = np.stack(split(lift.reshape(12 * m, slabs * 16)))
    gcos, gsin = wave(m, m, m)
    angle = np.arctan2(gsin, gcos)
    both = angle[:, None, :, None] + angle[None, :, None, :]
    cos2 = np.cos(both).reshape(m * m, m * m).T
    sin2 = np.sin(both).reshape(m * m, m * m).T
    forth = np.block([[cos2, sin2], [-sin2, cos2]]).astype(ml_dtypes.bfloat16)
    back = np.block([[cos2.T, -sin2.T], [sin2.T, cos2.T]]).astype(ml_dtypes.bfloat16)
    norm = float(m) ** (-1.5)
    freq = (np.arange(m) - m // 2) * (2.0 * math.pi / m)
    up = np.zeros((5, 3, m, 2, 4, 3, m))
    down = np.zeros((2, 3, 3, m, 4, 3, m))
    for c in range(3):
        up[0, c, :, 0, 0, c, :] = gcos * norm
        up[0, c, :, 1, 0, c, :] = -gsin * norm
        up[1, c, :, 0, 1, c, :] = gcos * norm
        up[1, c, :, 1, 1, c, :] = -gsin * norm
        up[2, c, :, 0, 0, c, :] = -gsin * norm * freq[None, :]
        up[2, c, :, 1, 0, c, :] = -gcos * norm * freq[None, :]
        for s in (2, 3):
            up[1 + s, c, :, 0, s, c, :] = -gsin * norm
            up[1 + s, c, :, 1, s, c, :] = -gcos * norm
        down[0, 0, c, :, 0, c, :] = gcos.T * norm
        down[1, 0, c, :, 0, c, :] = -gsin.T * norm
        down[0, 0, c, :, 1, c, :] = gsin.T * norm * freq[:, None]
        down[1, 0, c, :, 1, c, :] = gcos.T * norm * freq[:, None]
        for s in (1, 2):
            down[0, s, c, :, 1 + s, c, :] = gcos.T * norm
            down[1, s, c, :, 1 + s, c, :] = -gsin.T * norm
    up = up.reshape(15 * m, 24 * m).astype(ml_dtypes.bfloat16)
    down = down.reshape(18 * m, 12 * m).astype(ml_dtypes.bfloat16)
    whole = np.arange(m) - m // 2
    lanes_j, lanes_k = np.repeat(whole, m), np.tile(whole, m)
    squares = whole[:, None] ** 2 + (lanes_j**2 + lanes_k**2)[None, :]
    inertia = (1.0 + alpha_reg * squares) ** 2
    waves = np.stack([np.repeat(freq, m), np.tile(freq, m)])
    waves = np.concatenate([waves, np.zeros((6, m * m))])
    grid = np.concatenate([inertia, waves]).astype(np.float32)
    zfine = (np.concatenate([zcos.T, zsin.T]) * norm).astype(np.float32)
    ycos, ysin = wave(rows, rows, m)
    xcos, xsin = wave(cols, cols, m)
    spread = np.concatenate([np.tile(xcos.T, (m, 1)), np.tile(xsin.T, (m, 1))], axis=1)
    xs = np.stack(split(spread))
    yh, yl = split(np.concatenate([ycos, -ysin], axis=1))
    ys = np.concatenate([yh, yh, yl], axis=1)
    return lift, forth, back, up, down, grid, zfine, xs, ys


def force_kernel(
    tmpl, image, corner, frac, start, yt, xt,
    planes, vstart,
    near, tf, wf, wb, nearw, fb, acc, msg, cb, cs, db, ds,
    t_send, t_recv, w_send, w_recv, c_send, c_recv, cs_send, cs_recv,
    d_send, d_recv, ds_send, ds_recv,
):
    rows, cols = tmpl.shape
    height = rows // CHUNKS
    per = height // BLK
    phase = lax.axis_index("phase")
    slab = lax.axis_index("slab")
    slabs = lax.axis_size("slab")
    columns = slabs // ZLO
    low = slab % ZLO
    column = slab // ZLO
    spot = phase * ZLO + low
    has_down, has_up = slab > 0, slab < slabs - 1
    edge_down = jnp.logical_and(has_down, low == 0)
    edge_up = jnp.logical_and(has_up, low == ZLO - 1)
    other = (phase + 2) % 4
    t_phase = (jnp.where(edge_down, other, phase), jnp.where(edge_up, other, phase))

    def at(p, s):
        return {"phase": p, "slab": s}

    def mate(d):
        there = (spot + d) % 16
        return at(there // ZLO, slab - low + there % ZLO)

    def peer(d):
        return at(phase, ((column + d) % columns) * ZLO + low)

    barrier = pltpu.get_barrier_semaphore()

    def greet(d, carry):
        pl.semaphore_signal(barrier, inc=1, device_id=mate(d), device_id_type=MESH)
        pl.semaphore_signal(barrier, inc=1, device_id=peer(d), device_id_type=MESH)
        return carry

    for edge, step in ((edge_down, -1), (edge_up, 1)):
        @pl.when(edge)
        def _():
            pl.semaphore_signal(barrier, inc=1, device_id=at(phase, slab + step), device_id_type=MESH)
            pl.semaphore_signal(barrier, inc=1, device_id=at(other, slab + step), device_id_type=MESH)

    lax.fori_loop(1, 16, greet, 0)

    def spread(source, which):
        def body(r, carry):
            first = pl.multiple_of(r * BLK, BLK)
            value = source(first).astype(F32)
            there = pl.ds(pl.multiple_of(first + 8, 8), BLK)
            tf[3 * which, there, :] = pltpu.roll(value, 1, 1)
            tf[3 * which + 1, there, :] = value
            tf[3 * which + 2, there, :] = pltpu.roll(value, cols - 1, 1)
            return carry
        return body

    lax.fori_loop(0, rows // BLK, spread(lambda r: tmpl[pl.ds(r, BLK), :], 1), 0)
    edge_rows = jnp.zeros((8, cols), F32)
    for k in range(9):
        tf[k, 0:8, :] = edge_rows
        tf[k, rows + 8 : rows + 16, :] = edge_rows
    wf[0:8, :] = edge_rows
    wf[rows + 8 : rows + 16, :] = edge_rows
    cs[spot] = jnp.zeros((8, 128), F32)
    cs[spot, 0:6, 0:64] = start[...]

    @pl.when(jnp.logical_not(has_down))
    def _():
        near[0] = jnp.zeros((rows, cols), BF16)
        nearw[0] = jnp.zeros((rows, cols), BF16)

    @pl.when(jnp.logical_not(has_up))
    def _():
        near[1] = jnp.zeros((rows, cols), BF16)
        nearw[1] = jnp.zeros((rows, cols), BF16)

    pl.semaphore_wait(
        barrier, 30 + 2 * edge_down.astype(jnp.int32) + 2 * edge_up.astype(jnp.int32)
    )

    sides = ((0, has_down, -1), (1, has_up, 1))

    def t_copy(side, step, ch):
        part = pl.ds(ch * height, height)
        return pltpu.make_async_remote_copy(
            src_ref=tmpl.at[part], dst_ref=near.at[1 - side, part],
            send_sem=t_send.at[side, ch], recv_sem=t_recv.at[1 - side, ch],
            device_id=at(t_phase[side], slab + step), device_id_type=MESH,
        )

    def w_copy(side, step, ch):
        part = pl.ds(ch * height, height)
        return pltpu.make_async_remote_copy(
            src_ref=wb.at[part], dst_ref=nearw.at[1 - side, part],
            send_sem=w_send.at[side, ch], recv_sem=w_recv.at[1 - side, ch],
            device_id=at(phase, slab + step), device_id_type=MESH,
        )

    for ch in range(CHUNKS):
        for side, has, step in sides:
            @pl.when(has)
            def _():
                t_copy(side, step, ch).start()

    def first_start(d):
        return pltpu.make_async_remote_copy(
            src_ref=cs.at[spot], dst_ref=cs.at[spot],
            send_sem=cs_send.at[d], recv_sem=cs_recv.at[d],
            device_id=mate(d), device_id_type=MESH,
        )

    def first_plane(d):
        return pltpu.make_async_remote_copy(
            src_ref=cb.at[spot], dst_ref=cb.at[spot],
            send_sem=c_send.at[d], recv_sem=c_recv.at[d],
            device_id=mate(d), device_id_type=MESH,
        )

    def second_start(d):
        return pltpu.make_async_remote_copy(
            src_ref=ds.at[column], dst_ref=ds.at[column],
            send_sem=ds_send.at[d], recv_sem=ds_recv.at[d],
            device_id=peer(d), device_id_type=MESH,
        )

    def second_plane(d):
        return pltpu.make_async_remote_copy(
            src_ref=db.at[column], dst_ref=db.at[column],
            send_sem=d_send.at[d], recv_sem=d_recv.at[d],
            device_id=peer(d), device_id_type=MESH,
        )

    def start_all(copy):
        def body(d, carry):
            copy(d).start()
            return carry
        lax.fori_loop(1, 16, body, 0)

    def wait_all(copy):
        def body(d, carry):
            copy(d).wait()
            return carry
        lax.fori_loop(1, 16, body, 0)

    start_all(first_start)

    col = lax.broadcasted_iota(jnp.int32, (BLK, 128), 1)
    line = lax.broadcasted_iota(jnp.int32, (BLK, 128), 0)

    def warp_block(r, carry):
        first = pl.multiple_of(r * BLK, BLK)
        here = pl.ds(first, BLK)
        window = pl.ds(first, BLK + 16)
        for lt in range(cols // 128):
            lane = slice(lt * 128, lt * 128 + 128)
            code = corner[here, lane]
            fz = frac[0, here, lane].astype(F32)
            fy = frac[1, here, lane].astype(F32)
            fx = frac[2, here, lane].astype(F32)
            lifted = code >= 4
            ybit = jnp.where(line + first == 0, 2, jnp.where(line + first == rows - 1, 0, code & 2))
            same_y = ybit == 2
            xbit = code & 1
            if lt == 0:
                xbit = jnp.where(col == 0, 1, xbit)
            if lt == cols // 128 - 1:
                xbit = jnp.where(col == 127, 0, xbit)
            same_x = xbit == 1
            across = []
            for k in range(3):
                along = []
                for dy in range(3):
                    left, mid, right = (
                        tf[3 * k + s, window, lane][7 + dy : 7 + dy + BLK, :] for s in range(3)
                    )
                    lo = jnp.where(same_x, mid, left)
                    hi = jnp.where(same_x, right, mid)
                    along.append(lo + fx * (hi - lo))
                lo = jnp.where(same_y, along[1], along[0])
                hi = jnp.where(same_y, along[2], along[1])
                across.append(lo + fy * (hi - lo))
            lo = jnp.where(lifted, across[1], across[0])
            hi = jnp.where(lifted, across[2], across[1])
            value = (lo + fz * (hi - lo)).astype(BF16)
            wb[here, lane] = value
            wf[pl.ds(pl.multiple_of(first + 8, 8), BLK), lane] = value.astype(F32)
        return carry

    def arrive(ch):
        for side, has, step in sides:
            @pl.when(has)
            def _():
                t_copy(1 - side, step, ch).wait_recv()
        for which, slot in ((0, 0), (2, 1)):
            lax.fori_loop(
                ch * per, ch * per + per,
                spread(lambda r: near[slot, pl.ds(r, BLK), :], which), 0,
            )

    arrive(0)
    for ch in range(CHUNKS):
        if ch + 1 < CHUNKS:
            arrive(ch + 1)
        lax.fori_loop(ch * per, ch * per + per, warp_block, 0)
        for side, has, step in sides:
            @pl.when(has)
            def _():
                w_copy(side, step, ch).start()

    wait_all(first_start)
    for q in range(ZLO):
        mean = (cs[q] + cs[ZLO + q] + cs[2 * ZLO + q] + cs[3 * ZLO + q]) * 0.25
        ds[column, 8 * q : 8 * q + 8, :] = cs[phase * ZLO + q] - mean
    start_all(second_start)

    def flat_block(r, carry):
        first = pl.multiple_of(r * BLK, BLK)
        here = pl.ds(first, BLK)
        centre = wf[pl.ds(pl.multiple_of(first + 8, 8), BLK), :]
        rest = (image[here, :].astype(F32) - centre) * 0.5
        window = wf[pl.ds(first, BLK + 16), :]
        grad_y = window[9 : 9 + BLK, :] - window[7 : 7 + BLK, :]
        fb[1, here, :] = (rest * grad_y).astype(BF16)
        place = lax.broadcasted_iota(jnp.int32, (BLK, cols), 1)
        after = jnp.where(place == cols - 1, 0.0, pltpu.roll(centre, cols - 1, 1))
        before = jnp.where(place == 0, 0.0, pltpu.roll(centre, 1, 1))
        fb[2, here, :] = (rest * (after - before)).astype(BF16)
        return carry

    lax.fori_loop(0, rows // BLK, flat_block, 0)

    lane = lax.broadcasted_iota(jnp.int32, (KM, KM * KM), 1)
    own_j = lane // KM == lax.broadcasted_iota(jnp.int32, (KM, KM * KM), 0)

    def analyse(c):
        both = dot(yt[...], fb[c])
        acc[...] = both[0:32] + both[32:64]
        high, low_part = halves(acc[...])
        wide = dot(high, xt[0]) + dot(low_part, xt[0]) + dot(high, xt[1])
        real = wide[0:16, 0:256] + wide[16:32, 256:512]
        imag = wide[16:32, 0:256] - wide[0:16, 256:512]
        for part, value in ((0, real), (1, imag)):
            line_sum = jnp.sum(jnp.where(own_j, value, 0.0), axis=0, keepdims=True)
            at_row = 4 * c + 2 * part
            msg[at_row : at_row + 1, :] = line_sum[:, 0:128]
            msg[at_row + 1 : at_row + 2, :] = line_sum[:, 128:256]

    msg[8:16, :] = jnp.zeros((8, 128), F32)
    analyse(1)
    analyse(2)

    wait_all(second_start)
    from_slab = (
        lax.broadcasted_iota(jnp.int32, (slabs, KM * KM), 1) // 4
        == lax.broadcasted_iota(jnp.int32, (slabs, KM * KM), 0)
    ).astype(F32)
    quarter = lane % 4
    for c in range(6):
        block = jnp.concatenate(
            [ds[x, pl.ds(c, ZLO, stride=8), :] for x in range(columns)], axis=0
        )
        wide = lax.dot_general(
            block, from_slab, (((0,), (0,)), ((), ())),
            precision=HIGH, preferred_element_type=F32,
        )
        total = jnp.zeros((KM, KM * KM), F32)
        for q in range(4):
            total = jnp.where(quarter == q, wide[q * KM : q * KM + KM], total)
        vstart[c * KM : c * KM + KM, :] = total

    def deep_block(r, carry):
        first = pl.multiple_of(r * BLK, BLK)
        here = pl.ds(first, BLK)
        centre = wf[pl.ds(pl.multiple_of(first + 8, 8), BLK), :]
        rest = (image[here, :].astype(F32) - centre) * 0.5
        grad_z = nearw[1, here, :].astype(F32) - nearw[0, here, :].astype(F32)
        fb[0, here, :] = (rest * grad_z).astype(BF16)
        return carry

    for ch in range(CHUNKS):
        for side, has, step in sides:
            @pl.when(has)
            def _():
                w_copy(1 - side, step, ch).wait_recv()
        lax.fori_loop(ch * per, ch * per + per, deep_block, 0)
    analyse(0)

    cb[spot] = msg[...].astype(BF16)
    start_all(first_plane)
    wait_all(first_plane)
    for q in range(ZLO):
        values = [cb[p * ZLO + q].astype(F32) for p in range(4)]
        mean = (values[0] + values[1] + values[2] + values[3]) * 0.25
        own = cb[phase * ZLO + q].astype(F32)
        db[column, 16 * q : 16 * q + 16, :] = (own - mean).astype(BF16)
    start_all(second_plane)
    wait_all(second_plane)
    for x in range(columns):
        planes[64 * x : 64 * x + 64, :] = db[x]

    for ch in range(CHUNKS):
        for side, has, step in sides:
            @pl.when(has)
            def _():
                t_copy(side, step, ch).wait_send()
                w_copy(side, step, ch).wait_send()


def shoot_kernel(
    planes, vstart, lift, forth, back, up, down, grid, zfine, xs, ys, centred, velocity
):
    slab = lax.axis_index("slab")
    m = KM
    inertia = jnp.concatenate([grid[0:m, :]] * 3)
    kernel = 1.0 / inertia
    wave_y = grid[m : m + 1, :]
    wave_x = grid[m + 1 : m + 2, :]
    stacked = planes[...]
    out = dot(lift[0], stacked) + dot(lift[1], stacked)
    real = jnp.concatenate([out[0:48], out[96:144]], axis=1)
    imag = jnp.concatenate([out[48:96], out[144:192]], axis=1)
    vel_re = 0.5 * vstart[0:48, :] + step_size * kernel * real
    vel_im = 0.5 * vstart[48:96, :] + step_size * kernel * imag

    lane = lax.broadcasted_iota(jnp.int32, (m * m, 128), 1)
    mode = lax.broadcasted_iota(jnp.int32, (m * m, 128), 0)
    pick = (mode == 4 * slab + lane // m).astype(F32)
    taken = jnp.dot(
        jnp.concatenate([vel_re, vel_im]), pick, precision=HIGH, preferred_element_type=F32
    )
    diagonal = (
        lax.broadcasted_iota(jnp.int32, (m, 128), 1) % m
        == lax.broadcasted_iota(jnp.int32, (m, 128), 0)
    )
    for c in range(6):
        line = jnp.sum(jnp.where(diagonal, taken[c * m : c * m + m], 0.0), axis=0, keepdims=True)
        centred[c : c + 1, :] = line[:, 0 : 4 * m]

    for step in range(STEPS):
        inputs_re = jnp.concatenate([vel_re, inertia * vel_re, wave_y * vel_re, wave_x * vel_re])
        inputs_im = jnp.concatenate([vel_im, inertia * vel_im, wave_y * vel_im, wave_x * vel_im])
        inputs = jnp.concatenate([inputs_re, inputs_im], axis=1).astype(BF16)
        flat = dot(inputs, forth[...])
        tall = jnp.concatenate([flat[:, 0:256], flat[:, 256:512]]).astype(BF16)
        fields = dot(up[...], tall)

        def field(kind, c):
            return fields[kind * 48 + c * m : kind * 48 + c * m + m]

        speed = [field(0, c) for c in range(3)]
        momentum = [field(1, c) for c in range(3)]
        advect = [
            field(2 + i, 0) * momentum[0] + field(2 + i, 1) * momentum[1] + field(2 + i, 2) * momentum[2]
            for i in range(3)
        ]
        outer = [momentum[i] * speed[j] for j in range(3) for i in range(3)]
        products = jnp.concatenate(advect + outer).astype(BF16)
        half = dot(down[...], products)
        wide = jnp.concatenate([half[0:144], half[144:288]], axis=1).astype(BF16)
        spec = dot(wide, back[...])
        coad_re = spec[0:48, 0:256] - wave_y * spec[48:96, 256:512] - wave_x * spec[96:144, 256:512]
        coad_im = spec[0:48, 256:512] + wave_y * spec[48:96, 0:256] + wave_x * spec[96:144, 0:256]
        vel_re = vel_re - time_step * kernel * coad_re
        vel_im = vel_im - time_step * kernel * coad_im

    slabs = zfine.shape[1]
    chosen = (lax.broadcasted_iota(jnp.int32, (slabs, 256), 0) == slab).astype(F32)
    zwave = jnp.dot(zfine[...], chosen, precision=HIGH, preferred_element_type=F32)
    zcos, zsin = zwave[0:m], zwave[m : 2 * m]
    own_j = (
        lax.broadcasted_iota(jnp.int32, (m, m * m), 1) // m
        == lax.broadcasted_iota(jnp.int32, (m, m * m), 0)
    )
    rows_re, rows_im = [], []
    for c in range(3):
        re, im = vel_re[c * m : c * m + m], vel_im[c * m : c * m + m]
        plane_re = jnp.sum(re * zcos - im * zsin, axis=0, keepdims=True)
        plane_im = jnp.sum(re * zsin + im * zcos, axis=0, keepdims=True)
        rows_re.append(jnp.where(own_j, plane_re, 0.0))
        rows_im.append(jnp.where(own_j, plane_im, 0.0))
    high, low = halves(jnp.concatenate(rows_re + rows_im))
    wide = dot(high, xs[0]) + dot(low, xs[0]) + dot(high, xs[1])
    cols = wide.shape[1] // 2
    x_re = wide[0:48, 0:cols] - wide[48:96, cols:]
    x_im = wide[0:48, cols:] + wide[48:96, 0:cols]
    for c in range(3):
        pair = jnp.concatenate([x_re[c * m : c * m + m], x_im[c * m : c * m + m]])
        high, low = halves(pair)
        velocity[c] = dot(ys[...], jnp.concatenate([high, low, high])).astype(BF16)


def force_call(tmpl, image, corner, frac, start, slabs):
    rows, cols = tmpl.shape
    yt, xt = analysis_tables(rows, cols)
    columns = slabs // ZLO
    dma = pltpu.SemaphoreType.DMA
    whole = pl.BlockSpec(memory_space=VMEM)
    return pl.pallas_call(
        force_kernel,
        out_shape=(
            jax.ShapeDtypeStruct((slabs * 16, 128), BF16),
            jax.ShapeDtypeStruct((6 * KM, KM * KM), F32),
        ),
        in_specs=[whole] * 7,
        out_specs=(whole, whole),
        scratch_shapes=[
            VMEM((2, rows, cols), BF16),
            VMEM((9, rows + 16, cols), F32),
            VMEM((rows + 16, cols), F32),
            VMEM((rows, cols), BF16),
            VMEM((2, rows, cols), BF16),
            VMEM((3, rows, cols), BF16),
            VMEM((2 * KM, cols), F32),
            VMEM((16, 128), F32),
            VMEM((16, 16, 128), BF16),
            VMEM((16, 8, 128), F32),
            VMEM((columns, 64, 128), BF16),
            VMEM((columns, 32, 128), F32),
            dma((2, CHUNKS)), dma((2, CHUNKS)), dma((2, CHUNKS)), dma((2, CHUNKS)),
            dma((16,)), dma((16,)), dma((16,)), dma((16,)),
            dma((16,)), dma((16,)), dma((16,)), dma((16,)),
        ],
        compiler_params=pltpu.CompilerParams(
            collective_id=0, has_side_effects=True, vmem_limit_bytes=48 * 2**20
        ),
        name="force",
    )(tmpl, image, corner, frac, start, jnp.asarray(yt), jnp.asarray(xt))


def shoot_call(planes, vstart, slabs, rows, cols):
    tables = [jnp.asarray(t) for t in shooting_tables(slabs, rows, cols)]
    whole = pl.BlockSpec(memory_space=VMEM)
    return pl.pallas_call(
        shoot_kernel,
        out_shape=(
            jax.ShapeDtypeStruct((6, 4 * KM), F32),
            jax.ShapeDtypeStruct((3, rows, cols), BF16),
        ),
        in_specs=[whole] * (2 + len(tables)),
        out_specs=(whole, whole),
        compiler_params=pltpu.CompilerParams(vmem_limit_bytes=48 * 2**20),
        name="shoot",
    )(planes, vstart, *tables)


def local(template, phase_images, corner, fractions, start_modes):
    depth, rows, cols = template.shape
    slabs = lax.axis_size("slab")
    planes, vstart = force_call(
        template[0], phase_images[0, 0], corner[0, 0], fractions[0, :, 0], start_modes[0], slabs
    )
    centred, velocity = shoot_call(planes, vstart, slabs, rows, cols)
    return (centred[None], velocity[None, :, None])


def solution(mesh):
    placed = (
        P("slab", None, None),
        P("phase", "slab", None, None),
        P("phase", "slab", None, None),
        P("phase", None, "slab", None, None),
        P("phase", None, "slab"),
    )
    return jax.shard_map(
        local,
        mesh=mesh,
        in_specs=placed,
        out_specs=(P("phase", None, "slab"), P("phase", None, "slab", None, None)),
        check_vma=False,
    )
```

```python
import functools
import math

import ml_dtypes
import numpy as np

import jax
import jax.numpy as jnp
from jax import lax
from jax.experimental import pallas as pl
from jax.experimental.pallas import tpu as pltpu
from jax.sharding import PartitionSpec as P

KM = 16
STEPS = 2
ZLO = 4
T_ENDS = (96, 224, 320, 384)
W_ENDS = (64, 192, 304, 352, 384)
BLK = 16
EARLY_AT = 3
HIGH = lax.Precision.HIGHEST
MESH = pl.DeviceIdType.MESH
step_size = 0.5
alpha_reg = 0.002
time_step = 0.025
F32 = jnp.float32
BF16 = jnp.bfloat16
VMEM = pltpu.VMEM


def wave(count, length, modes):
    places = np.arange(count, dtype=np.int64)
    freq = np.arange(modes, dtype=np.int64) - modes // 2
    angle = np.mod(places[:, None] * freq[None, :], length) * (2.0 * math.pi / length)
    return np.cos(angle), np.sin(angle)


def split(table):
    table = np.asarray(table, np.float32)
    high = table.astype(ml_dtypes.bfloat16)
    low = (table - high.astype(np.float32)).astype(ml_dtypes.bfloat16)
    return high, low


def halves(value):
    high = value.astype(BF16)
    low = (value - high.astype(F32)).astype(BF16)
    return high, low


def dot(left, right):
    return jnp.dot(left, right, preferred_element_type=F32)


def analysis_tables(rows, cols):
    ycos, ysin = wave(rows, rows, KM)
    xcos, xsin = wave(cols, cols, KM)
    yt = np.concatenate(split(np.concatenate([ycos, -ysin], axis=1)), axis=1)
    spread = np.concatenate([np.tile(xcos, (1, KM)), np.tile(xsin, (1, KM))], axis=1)
    xt = np.stack(split(spread))
    return yt, xt


def shooting_tables(slabs, rows, cols):
    m = KM
    zcos, zsin = wave(slabs, slabs, m)
    scale = 1.0 / math.sqrt(rows * cols * slabs)
    lifts = []
    for comps, lines in ((1, 8), (2, 16)):
        lift = np.zeros((2, 2, comps, m, slabs, lines))
        for half in range(2):
            for comp in range(comps):
                real, imag = comp * 4 + half, comp * 4 + 2 + half
                lift[half, 0, comp, :, :, real] = zcos.T * scale
                lift[half, 0, comp, :, :, imag] = zsin.T * scale
                lift[half, 1, comp, :, :, imag] = zcos.T * scale
                lift[half, 1, comp, :, :, real] = -zsin.T * scale
        if comps == 1:
            for s in range(slabs):
                across = s - 1 if s % ZLO == 0 else s + 1
                if s % ZLO in (0, ZLO - 1) and 0 <= across < slabs:
                    lift[..., s, 4:8] = lift[..., across, 0:4]
        lifts.append(np.stack(split(lift.reshape(4 * comps * m, slabs * lines))))
    late, early = lifts
    sel = np.zeros((slabs, 16, 3, slabs, 4), ml_dtypes.bfloat16)
    for row in range(3):
        for s in range(slabs):
            sel[s, 8 + row, row, s, :] = 1
            sel[s, 11 + row, row, s, :] = 1
    sel = sel.reshape(slabs * 16, 12 * slabs)
    gcos, gsin = wave(m, m, m)
    angle = np.arctan2(gsin, gcos)
    both = angle[:, None, :, None] + angle[None, :, None, :]
    cos2 = np.cos(both).reshape(m * m, m * m).T
    sin2 = np.sin(both).reshape(m * m, m * m).T
    forth = np.block([[cos2, sin2], [-sin2, cos2]]).astype(ml_dtypes.bfloat16)
    back = np.block([[cos2.T, -sin2.T], [sin2.T, cos2.T]]).astype(ml_dtypes.bfloat16)
    norm = float(m) ** (-1.5)
    freq = (np.arange(m) - m // 2) * (2.0 * math.pi / m)
    up = np.zeros((5, 3, m, 2, 4, 3, m))
    down = np.zeros((2, 3, 3, m, 4, 3, m))
    for c in range(3):
        up[0, c, :, 0, 0, c, :] = gcos * norm
        up[0, c, :, 1, 0, c, :] = -gsin * norm
        up[1, c, :, 0, 1, c, :] = gcos * norm
        up[1, c, :, 1, 1, c, :] = -gsin * norm
        up[2, c, :, 0, 0, c, :] = -gsin * norm * freq[None, :]
        up[2, c, :, 1, 0, c, :] = -gcos * norm * freq[None, :]
        for s in (2, 3):
            up[1 + s, c, :, 0, s, c, :] = -gsin * norm
            up[1 + s, c, :, 1, s, c, :] = -gcos * norm
        down[0, 0, c, :, 0, c, :] = gcos.T * norm
        down[1, 0, c, :, 0, c, :] = -gsin.T * norm
        down[0, 0, c, :, 1, c, :] = gsin.T * norm * freq[:, None]
        down[1, 0, c, :, 1, c, :] = gcos.T * norm * freq[:, None]
        for s in (1, 2):
            down[0, s, c, :, 1 + s, c, :] = gcos.T * norm
            down[1, s, c, :, 1 + s, c, :] = -gsin.T * norm
    up = up.reshape(15 * m, 24 * m).astype(ml_dtypes.bfloat16)
    down = down.reshape(18 * m, 12 * m).astype(ml_dtypes.bfloat16)
    whole = np.arange(m) - m // 2
    lanes_j, lanes_k = np.repeat(whole, m), np.tile(whole, m)
    squares = whole[:, None] ** 2 + (lanes_j**2 + lanes_k**2)[None, :]
    inertia = (1.0 + alpha_reg * squares) ** 2
    waves = np.stack([np.repeat(freq, m), np.tile(freq, m)])
    waves = np.concatenate([waves, np.zeros((6, m * m))])
    grid = np.concatenate([inertia, waves]).astype(np.float32)
    zfine = (np.concatenate([zcos.T, zsin.T]) * norm).astype(np.float32)
    ycos, ysin = wave(rows, rows, m)
    xcos, xsin = wave(cols, cols, m)
    spread = np.concatenate([np.tile(xcos.T, (m, 1)), np.tile(xsin.T, (m, 1))], axis=1)
    xs = np.stack(split(spread))
    yh, yl = split(np.concatenate([ycos, -ysin], axis=1))
    ys = np.concatenate([yh, yh, yl], axis=1)
    return sel, late, early, forth, back, up, down, grid, zfine, xs, ys


def flash_kernel(
    tmpl_hbm, image_hbm, corner_hbm, frac_hbm, start_hbm, yt_hbm, xt_hbm, sel_hbm, late_hbm, early_hbm, forth_hbm, back_hbm,
    up_hbm, down_hbm, grid_hbm, zfine_hbm, xs_hbm,
    centred, pairs,
    tmpl, image, corner, frac, start, yt, xt, sel, late, early, forth, back, up, down, grid, zfine, xs,
    near, tf, wf, wb, nearw, neari, fb, acc, msg, cb, db, cb_early, db_early,
    load_sem, t_send, t_recv, f_send, f_recv, w_send, w_recv, i_send, i_recv, c_send, c_recv,
    d_send, d_recv, ce_send, ce_recv, de_send, de_recv,
):
    rows, cols = tmpl.shape
    t_parts = [(a * rows // 384, b * rows // 384) for a, b in zip((0,) + T_ENDS, T_ENDS)]
    w_parts = [(a * rows // 384, b * rows // 384) for a, b in zip((0,) + W_ENDS, W_ENDS)]
    phase = lax.axis_index("phase")
    slab = lax.axis_index("slab")
    slabs = lax.axis_size("slab")
    columns = slabs // ZLO
    low = slab % ZLO
    column = slab // ZLO
    spot = phase * ZLO + low
    has_down, has_up = slab > 0, slab < slabs - 1
    edge_down = jnp.logical_and(has_down, low == 0)
    edge_up = jnp.logical_and(has_up, low == ZLO - 1)
    other = (phase + 2) % 4
    core = phase % 2
    sibling = phase + 1 - 2 * core
    t_phase = (jnp.where(edge_down, other, phase), jnp.where(edge_up, other, phase))

    def at(p, s):
        return {"phase": p, "slab": s}

    def mate(d):
        there = (spot + d) % 16
        return at(there // ZLO, slab - low + there % ZLO)

    def peer(d):
        return at(phase, ((column + d) % columns) * ZLO + low)

    barrier = pltpu.get_barrier_semaphore()

    def greet(d, carry):
        pl.semaphore_signal(barrier, inc=1, device_id=mate(d), device_id_type=MESH)
        pl.semaphore_signal(barrier, inc=1, device_id=peer(d), device_id_type=MESH)
        return carry

    for edge, step in ((edge_down, -1), (edge_up, 1)):
        @pl.when(edge)
        def _():
            pl.semaphore_signal(barrier, inc=1, device_id=at(phase, slab + step), device_id_type=MESH)
            pl.semaphore_signal(barrier, inc=1, device_id=at(other, slab + step), device_id_type=MESH)

    lax.fori_loop(1, 16, greet, 0)

    loads = [
        pltpu.make_async_copy(source, target, load_sem.at[i])
        for i, (source, target) in enumerate((
            (tmpl_hbm, tmpl), (start_hbm, start), (corner_hbm, corner), (frac_hbm, frac), (image_hbm, image),
            (yt_hbm, yt), (xt_hbm, xt), (sel_hbm, sel), (late_hbm, late), (early_hbm, early), (forth_hbm, forth), (back_hbm, back),
            (up_hbm, up), (down_hbm, down), (grid_hbm, grid), (zfine_hbm, zfine), (xs_hbm, xs),
        ))
    ]
    for load in loads:
        load.start()

    pl.semaphore_wait(
        barrier, 30 + 2 * edge_down.astype(jnp.int32) + 2 * edge_up.astype(jnp.int32)
    )

    sides = ((0, has_down, -1), (1, has_up, 1))

    def t_rows(ch, which):
        first, last = t_parts[ch]
        size = (last - first) // 2
        return pl.ds(pl.multiple_of(first + which * size, 16), size)

    def t_copy(side, step, ch):
        part = t_rows(ch, core)
        return pltpu.make_async_remote_copy(
            src_ref=tmpl_hbm.at[part], dst_ref=near.at[1 - side, part],
            send_sem=t_send.at[side, ch], recv_sem=t_recv.at[1 - side, ch],
            device_id=at(t_phase[side], slab + step), device_id_type=MESH,
        )

    def f_copy(slot, ch, which):
        part = t_rows(ch, which)
        return pltpu.make_async_remote_copy(
            src_ref=near.at[slot, part], dst_ref=near.at[slot, part],
            send_sem=f_send.at[slot, ch], recv_sem=f_recv.at[slot, ch],
            device_id=at(sibling, slab), device_id_type=MESH,
        )

    def w_copy(side, step, ch):
        first, last = w_parts[ch]
        part = pl.ds(first, last - first)
        return pltpu.make_async_remote_copy(
            src_ref=wb.at[part], dst_ref=nearw.at[1 - side, part],
            send_sem=w_send.at[side, ch], recv_sem=w_recv.at[1 - side, ch],
            device_id=at(phase, slab + step), device_id_type=MESH,
        )

    def in_first(ch):
        return w_parts[ch][1] <= rows // 2

    def sends(side, ch):
        if side:
            return has_up if in_first(ch) else jnp.logical_and(has_up, low != ZLO - 1)
        return jnp.logical_and(has_down, low != 0) if in_first(ch) else has_down

    def receives(slot, ch):
        if slot:
            return jnp.logical_and(has_up, low != ZLO - 1) if in_first(ch) else has_up
        return has_down if in_first(ch) else jnp.logical_and(has_down, low != 0)

    def i_copy(side, step):
        part = pl.ds(0 if side else rows // 2, rows // 2)
        return pltpu.make_async_remote_copy(
            src_ref=image_hbm.at[part], dst_ref=neari.at[part],
            send_sem=i_send.at[0], recv_sem=i_recv.at[0],
            device_id=at(phase, slab + step), device_id_type=MESH,
        )

    for ch in range(len(t_parts)):
        for side, has, step in sides:
            @pl.when(has)
            def _():
                t_copy(side, step, ch).start()

    edges = ((0, edge_down, -1), (1, edge_up, 1))
    for side, edge, step in edges:
        @pl.when(edge)
        def _():
            i_copy(side, step).start()

    def spread(source, which):
        def body(r, carry):
            first = pl.multiple_of(r * BLK, BLK)
            value = source(first).astype(F32)
            there = pl.ds(pl.multiple_of(first + 8, 8), BLK)
            tf[3 * which, there, :] = pltpu.roll(value, 1, 1)
            tf[3 * which + 1, there, :] = value
            tf[3 * which + 2, there, :] = pltpu.roll(value, cols - 1, 1)
            return carry
        return body

    loads[0].wait()
    lax.fori_loop(0, rows // BLK, spread(lambda r: tmpl[pl.ds(r, BLK), :], 1), 0, unroll=6)
    edge_rows = jnp.zeros((8, cols), F32)
    for k in range(9):
        tf[k, 0:8, :] = edge_rows
        tf[k, rows + 8 : rows + 16, :] = edge_rows
    wf[0:8, :] = edge_rows
    wf[rows + 8 : rows + 16, :] = edge_rows
    middle = rows // 2
    is_edge = jnp.logical_or(edge_down, edge_up)

    @pl.when(jnp.logical_not(has_down))
    def _():
        near[0] = jnp.zeros((rows, cols), BF16)
        nearw[0] = jnp.zeros((rows, cols), BF16)

    @pl.when(jnp.logical_not(has_up))
    def _():
        near[1] = jnp.zeros((rows, cols), BF16)
        nearw[1] = jnp.zeros((rows, cols), BF16)

    @pl.when(edge_down)
    def _():
        nearw[0, middle:rows, :] = jnp.zeros((middle, cols), BF16)

    @pl.when(edge_up)
    def _():
        nearw[1, 0:middle, :] = jnp.zeros((middle, cols), BF16)

    @pl.when(jnp.logical_not(is_edge))
    def _():
        fb[3] = jnp.zeros((rows, cols), BF16)

    def first_plane(d):
        return pltpu.make_async_remote_copy(
            src_ref=cb.at[spot], dst_ref=cb.at[spot],
            send_sem=c_send.at[0], recv_sem=c_recv.at[0],
            device_id=mate(d), device_id_type=MESH,
        )

    def second_plane(d):
        return pltpu.make_async_remote_copy(
            src_ref=db.at[column], dst_ref=db.at[column],
            send_sem=d_send.at[0], recv_sem=d_recv.at[0],
            device_id=peer(d), device_id_type=MESH,
        )

    def first_early(d):
        return pltpu.make_async_remote_copy(
            src_ref=cb_early.at[spot], dst_ref=cb_early.at[spot],
            send_sem=ce_send.at[0], recv_sem=ce_recv.at[0],
            device_id=mate(d), device_id_type=MESH,
        )

    def second_early(d):
        return pltpu.make_async_remote_copy(
            src_ref=db_early.at[column], dst_ref=db_early.at[column],
            send_sem=de_send.at[0], recv_sem=de_recv.at[0],
            device_id=peer(d), device_id_type=MESH,
        )

    def start_all(copy):
        def body(d, carry):
            copy(d).start()
            return carry
        lax.fori_loop(1, 16, body, 0)

    def all_of(buffer, send, recv):
        part = buffer.at[pl.ds(0, 15)]
        return pltpu.make_async_remote_copy(
            src_ref=part, dst_ref=part, send_sem=send.at[0], recv_sem=recv.at[0],
            device_id=mate(1), device_id_type=MESH,
        )

    every = {
        "first_plane": all_of(cb, c_send, c_recv),
        "second_plane": all_of(db, d_send, d_recv),
        "first_early": all_of(cb_early, ce_send, ce_recv), "second_early": all_of(db_early, de_send, de_recv),
    }


    col = lax.broadcasted_iota(jnp.int32, (BLK, 128), 1)
    line = lax.broadcasted_iota(jnp.int32, (BLK, 128), 0)

    def warp_block(r, carry):
        first = pl.multiple_of(r * BLK, BLK)
        here = pl.ds(first, BLK)
        window = pl.ds(first, BLK + 16)
        for lt in range(cols // 128):
            lane = slice(lt * 128, lt * 128 + 128)
            code = corner[here, lane]
            fz = frac[0, here, lane].astype(F32)
            fy = frac[1, here, lane].astype(F32)
            fx = frac[2, here, lane].astype(F32)
            lifted = code >= 4
            ybit = jnp.where(line + first == 0, 2, jnp.where(line + first == rows - 1, 0, code & 2))
            same_y = ybit == 2
            xbit = code & 1
            if lt == 0:
                xbit = jnp.where(col == 0, 1, xbit)
            if lt == cols // 128 - 1:
                xbit = jnp.where(col == 127, 0, xbit)
            same_x = xbit == 1
            across = []
            for k in range(3):
                along = []
                for dy in range(3):
                    left, mid, right = (
                        tf[3 * k + s, window, lane][7 + dy : 7 + dy + BLK, :] for s in range(3)
                    )
                    lo = jnp.where(same_x, mid, left)
                    hi = jnp.where(same_x, right, mid)
                    along.append(lo + fx * (hi - lo))
                lo = jnp.where(same_y, along[1], along[0])
                hi = jnp.where(same_y, along[2], along[1])
                across.append(lo + fy * (hi - lo))
            lo = jnp.where(lifted, across[1], across[0])
            hi = jnp.where(lifted, across[2], across[1])
            value = (lo + fz * (hi - lo)).astype(BF16)
            wb[here, lane] = value
            wf[pl.ds(pl.multiple_of(first + 8, 8), BLK), lane] = value.astype(F32)
        return carry

    def arrive(ch):
        for side, has, step in sides:
            @pl.when(has)
            def _():
                t_copy(1 - side, step, ch).wait_recv()
                f_copy(side, ch, core).start()

    def unpack(ch):
        for side, has, step in sides:
            @pl.when(has)
            def _():
                f_copy(side, ch, 1 - core).wait_recv()
        first, last = t_parts[ch]
        for which, slot in ((0, 0), (2, 1)):
            lax.fori_loop(
                first // BLK, last // BLK,
                spread(lambda r: near[slot, pl.ds(r, BLK), :], which), 0, unroll=6,
            )

    for load in loads[2:4]:
        load.wait()
    arrive(0)
    for ch, (first, last) in enumerate(w_parts):
        if ch < len(t_parts):
            unpack(ch)
        if ch + 1 < len(t_parts):
            arrive(ch + 1)
        lax.fori_loop(first // BLK, last // BLK, warp_block, 0, unroll=2)
        for side, has, step in sides:
            @pl.when(sends(side, ch))
            def _():
                w_copy(side, step, ch).start()

    for load in loads[4:7]:
        load.wait()

    def flat_block(r, carry):
        first = pl.multiple_of(r * BLK, BLK)
        here = pl.ds(first, BLK)
        centre = wf[pl.ds(pl.multiple_of(first + 8, 8), BLK), :]
        rest = (image[here, :].astype(F32) - centre) * 0.5
        window = wf[pl.ds(first, BLK + 16), :]
        grad_y = window[9 : 9 + BLK, :] - window[7 : 7 + BLK, :]
        fb[1, here, :] = (rest * grad_y).astype(BF16)
        place = lax.broadcasted_iota(jnp.int32, (BLK, cols), 1)
        after = jnp.where(place == cols - 1, 0.0, pltpu.roll(centre, cols - 1, 1))
        before = jnp.where(place == 0, 0.0, pltpu.roll(centre, 1, 1))
        fb[2, here, :] = (rest * (after - before)).astype(BF16)
        return carry

    lax.fori_loop(0, rows // BLK, flat_block, 0, unroll=4)

    lane = lax.broadcasted_iota(jnp.int32, (KM, KM * KM), 1)
    own_j = lane // KM == lax.broadcasted_iota(jnp.int32, (KM, KM * KM), 0)

    def along_y(c, first, last):
        return lax.dot_general(
            yt[first:last, :], fb[c, first:last, :], (((0,), (0,)), ((), ())), preferred_element_type=F32
        )

    def analyse(at_rows, sums):
        high, low_part = halves(jnp.concatenate([both[0:32] + both[32:64] for both in sums]))
        wide = dot(high, xt[0]) + dot(low_part, xt[0]) + dot(high, xt[1])
        for n, first in enumerate(at_rows):
            even, odd = wide[32 * n : 32 * n + 16], wide[32 * n + 16 : 32 * n + 32]
            real = even[:, 0:256] + odd[:, 256:512]
            imag = odd[:, 0:256] - even[:, 256:512]
            for part, value in ((0, real), (1, imag)):
                line_sum = jnp.sum(jnp.where(own_j, value, 0.0), axis=0, keepdims=True)
                at_row = first + 2 * part
                msg[at_row : at_row + 1, :] = line_sum[:, 0:128]
                msg[at_row + 1 : at_row + 2, :] = line_sum[:, 128:256]

    msg[8:16, :] = jnp.zeros((8, 128), F32)
    loads[1].wait()
    for c in range(6):
        high, low_part = halves(start[c])
        lanes = slice(64 * (c // 3), 64 * (c // 3) + 64)
        msg[8 + c % 3 : 9 + c % 3, lanes] = high.astype(F32)
        msg[11 + c % 3 : 12 + c % 3, lanes] = low_part.astype(F32)
    analyse((0, 4), (along_y(1, 0, rows), along_y(2, 0, rows)))
    cb_early[spot] = msg[...].astype(BF16)
    start_all(first_early)

    def centred_of(buffer, q):
        values = [buffer[p * ZLO + q].astype(F32) for p in range(4)]
        mean = (values[0] + values[1] + values[2] + values[3]) * 0.25
        return buffer[phase * ZLO + q].astype(F32) - mean

    def deep_block(r, carry):
        first = pl.multiple_of(r * BLK, BLK)
        here = pl.ds(first, BLK)
        centre = wf[pl.ds(pl.multiple_of(first + 8, 8), BLK), :]
        rest = (image[here, :].astype(F32) - centre) * 0.5
        grad_z = nearw[1, here, :].astype(F32) - nearw[0, here, :].astype(F32)
        fb[0, here, :] = (rest * grad_z).astype(BF16)
        return carry

    def across_block(slot):
        def body(r, carry):
            first = pl.multiple_of(r * BLK, BLK)
            here = pl.ds(first, BLK)
            mine = wf[pl.ds(pl.multiple_of(first + 8, 8), BLK), :] * (-0.5 if slot else 0.5)
            rest = neari[here, :].astype(F32) - nearw[slot, here, :].astype(F32)
            fb[3, here, :] = (rest * mine).astype(BF16)
            return carry
        return body

    def deep(ch):
        first, last = w_parts[ch]
        for side, has, step in sides:
            @pl.when(receives(side, ch))
            def _():
                w_copy(1 - side, step, ch).wait_recv()
        lax.fori_loop(first // BLK, last // BLK, deep_block, 0, unroll=True)

        slot = 0 if in_first(ch) else 1

        @pl.when(edge_down if in_first(ch) else edge_up)
        def _():
            lax.fori_loop(first // BLK, last // BLK, across_block(slot), 0, unroll=True)

        part = along_y(0, first, last)
        if ch == 0:
            acc[...] = part
        else:
            acc[...] += part

    for side, edge, step in edges:
        @pl.when(edge)
        def _():
            i_copy(1 - side, step).wait_recv()
    for ch in range(EARLY_AT):
        deep(ch)
    every["first_early"].wait_recv()
    for q in range(ZLO):
        value = centred_of(cb_early, q)
        high, low_part = halves(value[8:11] + value[11:14])
        msg[0:8, :] = value[0:8]
        msg[8:11, :] = high.astype(F32)
        msg[11:14, :] = low_part.astype(F32)
        db_early[column, 16 * q : 16 * q + 16, :] = msg[...].astype(BF16)
    start_all(second_early)
    for ch in range(EARLY_AT, len(w_parts)):
        deep(ch)
    start_row = pl.multiple_of(jnp.where(edge_up, middle, 0), 16)
    beyond = lax.dot_general(
        yt[pl.ds(start_row, middle), :], fb[3, pl.ds(start_row, middle), :],
        (((0,), (0,)), ((), ())), preferred_element_type=F32,
    )
    analyse((0, 4), (acc[...], beyond))

    cb[spot] = msg[...].astype(BF16)
    start_all(first_plane)
    for load in loads[7:]:
        load.wait()
    chosen = (lax.broadcasted_iota(jnp.int32, (slabs, 256), 0) == slab).astype(F32)
    zwave = jnp.dot(zfine[...], chosen, precision=HIGH, preferred_element_type=F32)
    zcos, zsin = zwave[0:KM], zwave[KM : 2 * KM]
    every["second_early"].wait_recv()
    stacked = jnp.concatenate([db_early[x] for x in range(columns)])
    out_early = dot(early[0], stacked) + dot(early[1], stacked)
    wide = lax.dot_general(stacked, sel[...], (((0,), (0,)), ((), ())), preferred_element_type=F32)
    starts = []
    for c in range(6):
        lanes = slice(256 * (c % 3), 256 * (c % 3) + 256)
        total = jnp.zeros((KM, KM * KM), F32)
        for q in range(4):
            first = 64 * (c // 3) + KM * q
            total = jnp.where(lane % 4 == q, wide[first : first + KM, lanes], total)
        starts.append(total)
    every["first_plane"].wait_recv()
    db[column] = jnp.concatenate([centred_of(cb, q)[0:8] for q in range(ZLO)]).astype(BF16)
    start_all(second_plane)
    every["second_plane"].wait_recv()
    m = KM
    inertia = jnp.concatenate([grid[0:m, :]] * 3)
    kernel = 1.0 / inertia
    wave_y = grid[m : m + 1, :]
    wave_x = grid[m + 1 : m + 2, :]
    stacked = jnp.concatenate([db[x] for x in range(columns)])
    out = dot(late[0], stacked) + dot(late[1], stacked)

    def modes_of(part):
        sides_of = [
            jnp.concatenate([
                out[32 * half + 16 * part : 32 * half + 16 * part + 16],
                out_early[64 * half + 32 * part : 64 * half + 32 * part + 32],
            ])
            for half in range(2)
        ]
        return jnp.concatenate(sides_of, axis=1)

    real, imag = modes_of(0), modes_of(1)
    vel_re = 0.5 * jnp.concatenate(starts[0:3]) + step_size * kernel * real
    vel_im = 0.5 * jnp.concatenate(starts[3:6]) + step_size * kernel * imag

    lane = lax.broadcasted_iota(jnp.int32, (m * m, 128), 1)
    mode = lax.broadcasted_iota(jnp.int32, (m * m, 128), 0)
    pick = (mode == 4 * slab + lane // m).astype(F32)
    taken = jnp.dot(
        jnp.concatenate([vel_re, vel_im]), pick, precision=HIGH, preferred_element_type=F32
    )
    diagonal = (
        lax.broadcasted_iota(jnp.int32, (m, 128), 1) % m
        == lax.broadcasted_iota(jnp.int32, (m, 128), 0)
    )
    for c in range(6):
        line = jnp.sum(jnp.where(diagonal, taken[c * m : c * m + m], 0.0), axis=0, keepdims=True)
        centred[c] = line[:, 0 : 4 * m]

    for step in range(STEPS):
        inputs_re = jnp.concatenate([vel_re, inertia * vel_re, wave_y * vel_re, wave_x * vel_re])
        inputs_im = jnp.concatenate([vel_im, inertia * vel_im, wave_y * vel_im, wave_x * vel_im])
        inputs = jnp.concatenate([inputs_re, inputs_im], axis=1).astype(BF16)
        flat = dot(inputs, forth[...])
        tall = jnp.concatenate([flat[:, 0:256], flat[:, 256:512]]).astype(BF16)
        fields = dot(up[...], tall)

        def field(kind, c):
            return fields[kind * 48 + c * m : kind * 48 + c * m + m]

        speed = [field(0, c) for c in range(3)]
        momentum = [field(1, c) for c in range(3)]
        advect = [
            field(2 + i, 0) * momentum[0] + field(2 + i, 1) * momentum[1] + field(2 + i, 2) * momentum[2]
            for i in range(3)
        ]
        outer = [momentum[i] * speed[j] for j in range(3) for i in range(3)]
        products = jnp.concatenate(advect + outer).astype(BF16)
        half = dot(down[...], products)
        wide = jnp.concatenate([half[0:144], half[144:288]], axis=1).astype(BF16)
        spec = dot(wide, back[...])
        coad_re = spec[0:48, 0:256] - wave_y * spec[48:96, 256:512] - wave_x * spec[96:144, 256:512]
        coad_im = spec[0:48, 256:512] + wave_y * spec[48:96, 0:256] + wave_x * spec[96:144, 0:256]
        vel_re = vel_re - time_step * kernel * coad_re
        vel_im = vel_im - time_step * kernel * coad_im

    rows_re, rows_im = [], []
    for c in range(3):
        re, im = vel_re[c * m : c * m + m], vel_im[c * m : c * m + m]
        plane_re = jnp.sum(re * zcos - im * zsin, axis=0, keepdims=True)
        plane_im = jnp.sum(re * zsin + im * zcos, axis=0, keepdims=True)
        rows_re.append(jnp.where(own_j, plane_re, 0.0))
        rows_im.append(jnp.where(own_j, plane_im, 0.0))
    high, low_part = halves(jnp.concatenate(rows_re + rows_im))
    wide = dot(high, xs[0]) + dot(low_part, xs[0]) + dot(high, xs[1])
    x_re = wide[0:48, 0:cols] - wide[48:96, cols:]
    x_im = wide[0:48, cols:] + wide[48:96, 0:cols]
    for c in range(3):
        pair = jnp.concatenate([x_re[c * m : c * m + m], x_im[c * m : c * m + m]])
        high, low_part = halves(pair)
        pairs[c] = jnp.concatenate([high, low_part, high])

    for side, has, step in sides:
        @pl.when(has)
        def _():
            for ch in range(len(t_parts)):
                t_copy(side, step, ch).wait_send()
                f_copy(side, ch, core).wait_send()
        for ch in range(len(w_parts)):
            @pl.when(sends(side, ch))
            def _():
                w_copy(side, step, ch).wait_send()
    for side, edge, step in edges:
        @pl.when(edge)
        def _():
            i_copy(side, step).wait_send()
    for copies in every.values():
        copies.wait_send()


def synth_kernel(pairs, modes, ys, centred, velocity_hbm, velocity, out_sem):
    centred[...] = modes[...]
    copies = [
        pltpu.make_async_copy(velocity.at[c], velocity_hbm.at[c], out_sem.at[c]) for c in range(3)
    ]
    for c in range(3):
        velocity[c] = dot(ys[...], pairs[c]).astype(BF16)
        copies[c].start()
    for copy in copies:
        copy.wait()


def flash_call(tmpl, image, corner, frac, start, slabs):
    rows, cols = tmpl.shape
    tables = [jnp.asarray(t) for t in analysis_tables(rows, cols) + shooting_tables(slabs, rows, cols)]
    inputs = [tmpl, image, corner, frac, start] + tables[:-1]
    columns = slabs // ZLO
    dma = pltpu.SemaphoreType.DMA
    any_space = pl.BlockSpec(memory_space=pl.ANY)
    return pl.pallas_call(
        flash_kernel,
        out_shape=(
            jax.ShapeDtypeStruct((6, 1, 4 * KM), F32),
            jax.ShapeDtypeStruct((3, 6 * KM, cols), BF16),
        ),
        in_specs=[any_space] * len(inputs),
        out_specs=(pl.BlockSpec(memory_space=VMEM),) * 2,
        scratch_shapes=[VMEM(x.shape, x.dtype) for x in inputs] + [
            VMEM((2, rows, cols), BF16),
            VMEM((9, rows + 16, cols), F32),
            VMEM((rows + 16, cols), F32),
            VMEM((rows, cols), BF16),
            VMEM((2, rows, cols), BF16),
            VMEM((rows, cols), BF16),
            VMEM((4, rows, cols), BF16),
            VMEM((4 * KM, cols), F32),
            VMEM((16, 128), F32),
            VMEM((16, 16, 128), BF16),
            VMEM((columns, 32, 128), BF16),
            VMEM((16, 16, 128), BF16),
            VMEM((columns, 64, 128), BF16),
            dma((len(inputs),)),
            dma((2, len(T_ENDS))), dma((2, len(T_ENDS))), dma((2, len(T_ENDS))), dma((2, len(T_ENDS))),
            dma((2, len(W_ENDS))), dma((2, len(W_ENDS))), dma((1,)), dma((1,)),
            dma((1,)), dma((1,)), dma((1,)), dma((1,)),
            dma((1,)), dma((1,)), dma((1,)), dma((1,)),
        ],
        compiler_params=pltpu.CompilerParams(
            collective_id=0, has_side_effects=True, vmem_limit_bytes=54 * 2**20
        ),
        name="flash",
    )(*inputs), tables[-1]


def synth_call(pairs, modes, ys):
    rows, cols = ys.shape[0], pairs.shape[2]
    whole = pl.BlockSpec(memory_space=VMEM)
    return pl.pallas_call(
        synth_kernel,
        out_shape=(
            jax.ShapeDtypeStruct(modes.shape, F32),
            jax.ShapeDtypeStruct((3, rows, cols), BF16),
        ),
        in_specs=[whole] * 3,
        out_specs=(whole, pl.BlockSpec(memory_space=pl.ANY)),
        scratch_shapes=[VMEM((3, rows, cols), BF16), pltpu.SemaphoreType.DMA((3,))],
        compiler_params=pltpu.CompilerParams(vmem_limit_bytes=16 * 2**20),
        name="synth",
    )(pairs, modes, ys)


def local(template, phase_images, corner, fractions, start_modes):
    slabs = lax.axis_size("slab")
    start = jnp.transpose(start_modes, (1, 0, 2))
    (modes, pairs), ys = flash_call(
        template[0], phase_images[0, 0], corner[0, 0], fractions[0, :, 0], start, slabs
    )
    centred, velocity = synth_call(pairs, modes, ys)
    return (jnp.transpose(centred, (1, 0, 2)), velocity[None, :, None])


def solution(mesh):
    placed = (
        P("slab", None, None),
        P("phase", "slab", None, None),
        P("phase", "slab", None, None),
        P("phase", None, "slab", None, None),
        P("phase", None, "slab"),
    )
    return jax.shard_map(
        local,
        mesh=mesh,
        in_specs=placed,
        out_specs=(P("phase", None, "slab"), P("phase", None, "slab", None, None)),
        check_vma=False,
    )
```

```python
import functools
import math

import ml_dtypes
import numpy as np

import jax
import jax.numpy as jnp
from jax import lax
from jax.experimental import pallas as pl
from jax.experimental.pallas import tpu as pltpu
from jax.sharding import PartitionSpec as P

KM = 16
STEPS = 2
ZLO = 4
T_ENDS = (96, 224, 320, 384)
W_ENDS = (64, 192, 304, 352, 384)
BLK = 16
EARLY_AT = 3
HIGH = lax.Precision.HIGHEST
MESH = pl.DeviceIdType.MESH
step_size = 0.5
alpha_reg = 0.002
time_step = 0.025
F32 = jnp.float32
BF16 = jnp.bfloat16
VMEM = pltpu.VMEM


def wave(count, length, modes):
    places = np.arange(count, dtype=np.int64)
    freq = np.arange(modes, dtype=np.int64) - modes // 2
    angle = np.mod(places[:, None] * freq[None, :], length) * (2.0 * math.pi / length)
    return np.cos(angle), np.sin(angle)


def split(table):
    table = np.asarray(table, np.float32)
    high = table.astype(ml_dtypes.bfloat16)
    low = (table - high.astype(np.float32)).astype(ml_dtypes.bfloat16)
    return high, low


def halves(value):
    high = value.astype(BF16)
    low = (value - high.astype(F32)).astype(BF16)
    return high, low


def dot(left, right):
    return jnp.dot(left, right, preferred_element_type=F32)


def analysis_tables(rows, cols):
    ycos, ysin = wave(rows, rows, KM)
    xcos, xsin = wave(cols, cols, KM)
    yt = np.concatenate(split(np.concatenate([ycos, -ysin], axis=1)), axis=1)
    spread = np.concatenate([np.tile(xcos, (1, KM)), np.tile(xsin, (1, KM))], axis=1)
    xt = np.stack(split(spread))
    return yt, xt


def shooting_tables(slabs, rows, cols):
    m = KM
    zcos, zsin = wave(slabs, slabs, m)
    scale = 1.0 / math.sqrt(rows * cols * slabs)
    lifts = []
    for comps, lines in ((1, 8), (2, 16)):
        lift = np.zeros((2, 2, comps, m, slabs, lines))
        for half in range(2):
            for comp in range(comps):
                real, imag = comp * 4 + half, comp * 4 + 2 + half
                lift[half, 0, comp, :, :, real] = zcos.T * scale
                lift[half, 0, comp, :, :, imag] = zsin.T * scale
                lift[half, 1, comp, :, :, imag] = zcos.T * scale
                lift[half, 1, comp, :, :, real] = -zsin.T * scale
        if comps == 1:
            for s in range(slabs):
                across = s - 1 if s % ZLO == 0 else s + 1
                if s % ZLO in (0, ZLO - 1) and 0 <= across < slabs:
                    lift[..., s, 4:8] = lift[..., across, 0:4]
        lifts.append(np.stack(split(lift.reshape(4 * comps * m, slabs * lines))))
    late, early = lifts
    sel = np.zeros((slabs, 16, 3, slabs, 4), ml_dtypes.bfloat16)
    for row in range(3):
        for s in range(slabs):
            sel[s, 8 + row, row, s, :] = 1
            sel[s, 11 + row, row, s, :] = 1
    sel = sel.reshape(slabs * 16, 12 * slabs)
    gcos, gsin = wave(m, m, m)
    angle = np.arctan2(gsin, gcos)
    both = angle[:, None, :, None] + angle[None, :, None, :]
    cos2 = np.cos(both).reshape(m * m, m * m).T
    sin2 = np.sin(both).reshape(m * m, m * m).T
    forth = np.block([[cos2, sin2], [-sin2, cos2]]).astype(ml_dtypes.bfloat16)
    back = np.block([[cos2.T, -sin2.T], [sin2.T, cos2.T]]).astype(ml_dtypes.bfloat16)
    norm = float(m) ** (-1.5)
    freq = (np.arange(m) - m // 2) * (2.0 * math.pi / m)
    up = np.zeros((5, 3, m, 2, 4, 3, m))
    down = np.zeros((2, 3, 3, m, 4, 3, m))
    for c in range(3):
        up[0, c, :, 0, 0, c, :] = gcos * norm
        up[0, c, :, 1, 0, c, :] = -gsin * norm
        up[1, c, :, 0, 1, c, :] = gcos * norm
        up[1, c, :, 1, 1, c, :] = -gsin * norm
        up[2, c, :, 0, 0, c, :] = -gsin * norm * freq[None, :]
        up[2, c, :, 1, 0, c, :] = -gcos * norm * freq[None, :]
        for s in (2, 3):
            up[1 + s, c, :, 0, s, c, :] = -gsin * norm
            up[1 + s, c, :, 1, s, c, :] = -gcos * norm
        down[0, 0, c, :, 0, c, :] = gcos.T * norm
        down[1, 0, c, :, 0, c, :] = -gsin.T * norm
        down[0, 0, c, :, 1, c, :] = gsin.T * norm * freq[:, None]
        down[1, 0, c, :, 1, c, :] = gcos.T * norm * freq[:, None]
        for s in (1, 2):
            down[0, s, c, :, 1 + s, c, :] = gcos.T * norm
            down[1, s, c, :, 1 + s, c, :] = -gsin.T * norm
    up = up.reshape(15 * m, 24 * m).astype(ml_dtypes.bfloat16)
    down = down.reshape(18 * m, 12 * m).astype(ml_dtypes.bfloat16)
    whole = np.arange(m) - m // 2
    lanes_j, lanes_k = np.repeat(whole, m), np.tile(whole, m)
    squares = whole[:, None] ** 2 + (lanes_j**2 + lanes_k**2)[None, :]
    inertia = (1.0 + alpha_reg * squares) ** 2
    waves = np.stack([np.repeat(freq, m), np.tile(freq, m)])
    waves = np.concatenate([waves, np.zeros((6, m * m))])
    grid = np.concatenate([inertia, waves]).astype(np.float32)
    zfine = (np.concatenate([zcos.T, zsin.T]) * norm).astype(np.float32)
    ycos, ysin = wave(rows, rows, m)
    xcos, xsin = wave(cols, cols, m)
    spread = np.concatenate([np.tile(xcos.T, (m, 1)), np.tile(xsin.T, (m, 1))], axis=1)
    xs = np.stack(split(spread))
    yh, yl = split(np.concatenate([ycos, -ysin], axis=1))
    ys = np.concatenate([yh, yh, yl], axis=1)
    return sel, late, early, forth, back, up, down, grid, zfine, xs, ys


def flash_kernel(
    tmpl_hbm, image_hbm, corner_hbm, frac_hbm, start_hbm, yt_hbm, xt_hbm, sel_hbm, late_hbm, early_hbm, forth_hbm, back_hbm,
    up_hbm, down_hbm, grid_hbm, zfine_hbm, xs_hbm,
    centred, pairs,
    tmpl, image, corner, frac, start, yt, xt, sel, late, early, forth, back, up, down, grid, zfine, xs,
    near, tf, wf, wb, nearw, neari, fb, acc, msg, cb, db, cb_early, db_early,
    load_sem, t_send, t_recv, f_send, f_recv, w_send, w_recv, i_send, i_recv, c_send, c_recv,
    d_send, d_recv, ce_send, ce_recv, de_send, de_recv,
):
    rows, cols = tmpl.shape
    t_parts = [(a * rows // 384, b * rows // 384) for a, b in zip((0,) + T_ENDS, T_ENDS)]
    w_parts = [(a * rows // 384, b * rows // 384) for a, b in zip((0,) + W_ENDS, W_ENDS)]
    phase = lax.axis_index("phase")
    slab = lax.axis_index("slab")
    slabs = lax.axis_size("slab")
    columns = slabs // ZLO
    low = slab % ZLO
    column = slab // ZLO
    spot = phase * ZLO + low
    has_down, has_up = slab > 0, slab < slabs - 1
    edge_down = jnp.logical_and(has_down, low == 0)
    edge_up = jnp.logical_and(has_up, low == ZLO - 1)
    other = (phase + 2) % 4
    core = phase % 2
    sibling = phase + 1 - 2 * core
    t_phase = (jnp.where(edge_down, other, phase), jnp.where(edge_up, other, phase))

    def at(p, s):
        return {"phase": p, "slab": s}

    def mate(d):
        there = (spot + d) % 16
        return at(there // ZLO, slab - low + there % ZLO)

    def peer(d):
        return at(phase, ((column + d) % columns) * ZLO + low)

    barrier = pltpu.get_barrier_semaphore()

    def greet(d, carry):
        pl.semaphore_signal(barrier, inc=1, device_id=mate(d), device_id_type=MESH)
        pl.semaphore_signal(barrier, inc=1, device_id=peer(d), device_id_type=MESH)
        return carry

    for edge, step in ((edge_down, -1), (edge_up, 1)):
        @pl.when(edge)
        def _():
            pl.semaphore_signal(barrier, inc=1, device_id=at(phase, slab + step), device_id_type=MESH)
            pl.semaphore_signal(barrier, inc=1, device_id=at(other, slab + step), device_id_type=MESH)

    lax.fori_loop(1, 16, greet, 0)

    loads = [
        pltpu.make_async_copy(source, target, load_sem.at[i])
        for i, (source, target) in enumerate((
            (tmpl_hbm, tmpl), (start_hbm, start), (corner_hbm, corner), (frac_hbm, frac), (image_hbm, image),
            (yt_hbm, yt), (xt_hbm, xt), (sel_hbm, sel), (late_hbm, late), (early_hbm, early), (forth_hbm, forth), (back_hbm, back),
            (up_hbm, up), (down_hbm, down), (grid_hbm, grid), (zfine_hbm, zfine), (xs_hbm, xs),
        ))
    ]
    for load in loads:
        load.start()

    pl.semaphore_wait(
        barrier, 30 + 2 * edge_down.astype(jnp.int32) + 2 * edge_up.astype(jnp.int32)
    )

    sides = ((0, has_down, -1), (1, has_up, 1))

    def t_rows(ch, which):
        first, last = t_parts[ch]
        size = (last - first) // 2
        return pl.ds(pl.multiple_of(first + which * size, 16), size)

    def t_copy(side, step, ch):
        part = t_rows(ch, core)
        return pltpu.make_async_remote_copy(
            src_ref=tmpl_hbm.at[part], dst_ref=near.at[1 - side, part],
            send_sem=t_send.at[side, ch], recv_sem=t_recv.at[1 - side, ch],
            device_id=at(t_phase[side], slab + step), device_id_type=MESH,
        )

    def f_copy(slot, ch, which):
        part = t_rows(ch, which)
        return pltpu.make_async_remote_copy(
            src_ref=near.at[slot, part], dst_ref=near.at[slot, part],
            send_sem=f_send.at[slot, ch], recv_sem=f_recv.at[slot, ch],
            device_id=at(sibling, slab), device_id_type=MESH,
        )

    def w_copy(side, step, ch):
        first, last = w_parts[ch]
        part = pl.ds(first, last - first)
        return pltpu.make_async_remote_copy(
            src_ref=wb.at[part], dst_ref=nearw.at[1 - side, part],
            send_sem=w_send.at[side, ch], recv_sem=w_recv.at[1 - side, ch],
            device_id=at(phase, slab + step), device_id_type=MESH,
        )

    def in_first(ch):
        return w_parts[ch][1] <= rows // 2

    def sends(side, ch):
        if side:
            return has_up if in_first(ch) else jnp.logical_and(has_up, low != ZLO - 1)
        return jnp.logical_and(has_down, low != 0) if in_first(ch) else has_down

    def receives(slot, ch):
        if slot:
            return jnp.logical_and(has_up, low != ZLO - 1) if in_first(ch) else has_up
        return has_down if in_first(ch) else jnp.logical_and(has_down, low != 0)

    def i_copy(side, step):
        part = pl.ds(0 if side else rows // 2, rows // 2)
        return pltpu.make_async_remote_copy(
            src_ref=image_hbm.at[part], dst_ref=neari.at[part],
            send_sem=i_send.at[0], recv_sem=i_recv.at[0],
            device_id=at(phase, slab + step), device_id_type=MESH,
        )

    for ch in range(len(t_parts)):
        for side, has, step in sides:
            @pl.when(has)
            def _():
                t_copy(side, step, ch).start()

    edges = ((0, edge_down, -1), (1, edge_up, 1))

    def spread(source, which):
        def body(r, carry):
            first = pl.multiple_of(r * BLK, BLK)
            value = source(first).astype(F32)
            there = pl.ds(pl.multiple_of(first + 8, 8), BLK)
            tf[3 * which, there, :] = pltpu.roll(value, 1, 1)
            tf[3 * which + 1, there, :] = value
            tf[3 * which + 2, there, :] = pltpu.roll(value, cols - 1, 1)
            return carry
        return body

    loads[0].wait()
    lax.fori_loop(0, rows // BLK, spread(lambda r: tmpl[pl.ds(r, BLK), :], 1), 0, unroll=6)
    edge_rows = jnp.zeros((8, cols), F32)
    for k in range(9):
        tf[k, 0:8, :] = edge_rows
        tf[k, rows + 8 : rows + 16, :] = edge_rows
    wf[0:8, :] = edge_rows
    wf[rows + 8 : rows + 16, :] = edge_rows
    middle = rows // 2
    is_edge = jnp.logical_or(edge_down, edge_up)

    @pl.when(jnp.logical_not(has_down))
    def _():
        near[0] = jnp.zeros((rows, cols), BF16)
        nearw[0] = jnp.zeros((rows, cols), BF16)

    @pl.when(jnp.logical_not(has_up))
    def _():
        near[1] = jnp.zeros((rows, cols), BF16)
        nearw[1] = jnp.zeros((rows, cols), BF16)

    @pl.when(edge_down)
    def _():
        nearw[0, middle:rows, :] = jnp.zeros((middle, cols), BF16)

    @pl.when(edge_up)
    def _():
        nearw[1, 0:middle, :] = jnp.zeros((middle, cols), BF16)

    @pl.when(jnp.logical_not(is_edge))
    def _():
        fb[3] = jnp.zeros((rows, cols), BF16)

    def first_plane(d):
        return pltpu.make_async_remote_copy(
            src_ref=cb.at[spot], dst_ref=cb.at[spot],
            send_sem=c_send.at[0], recv_sem=c_recv.at[0],
            device_id=mate(d), device_id_type=MESH,
        )

    def second_plane(d):
        return pltpu.make_async_remote_copy(
            src_ref=db.at[column], dst_ref=db.at[column],
            send_sem=d_send.at[0], recv_sem=d_recv.at[0],
            device_id=peer(d), device_id_type=MESH,
        )

    def first_early(d):
        return pltpu.make_async_remote_copy(
            src_ref=cb_early.at[spot], dst_ref=cb_early.at[spot],
            send_sem=ce_send.at[0], recv_sem=ce_recv.at[0],
            device_id=mate(d), device_id_type=MESH,
        )

    def second_early(d):
        return pltpu.make_async_remote_copy(
            src_ref=db_early.at[column], dst_ref=db_early.at[column],
            send_sem=de_send.at[0], recv_sem=de_recv.at[0],
            device_id=peer(d), device_id_type=MESH,
        )

    def start_all(copy):
        def body(d, carry):
            copy(d).start()
            return carry
        lax.fori_loop(1, 16, body, 0)

    def all_of(buffer, send, recv):
        part = buffer.at[pl.ds(0, 15)]
        return pltpu.make_async_remote_copy(
            src_ref=part, dst_ref=part, send_sem=send.at[0], recv_sem=recv.at[0],
            device_id=mate(1), device_id_type=MESH,
        )

    every = {
        "first_plane": all_of(cb, c_send, c_recv),
        "second_plane": all_of(db, d_send, d_recv),
        "first_early": all_of(cb_early, ce_send, ce_recv), "second_early": all_of(db_early, de_send, de_recv),
    }


    col = lax.broadcasted_iota(jnp.int32, (BLK, 128), 1)
    line = lax.broadcasted_iota(jnp.int32, (BLK, 128), 0)

    def warp_block(r, carry):
        first = pl.multiple_of(r * BLK, BLK)
        here = pl.ds(first, BLK)
        window = pl.ds(first, BLK + 16)
        for lt in range(cols // 128):
            lane = slice(lt * 128, lt * 128 + 128)
            code = corner[here, lane]
            fz = frac[0, here, lane].astype(F32)
            fy = frac[1, here, lane].astype(F32)
            fx = frac[2, here, lane].astype(F32)
            lifted = code >= 4
            ybit = jnp.where(line + first == 0, 2, jnp.where(line + first == rows - 1, 0, code & 2))
            same_y = ybit == 2
            xbit = code & 1
            if lt == 0:
                xbit = jnp.where(col == 0, 1, xbit)
            if lt == cols // 128 - 1:
                xbit = jnp.where(col == 127, 0, xbit)
            same_x = xbit == 1
            across = []
            for k in range(3):
                along = []
                for dy in range(3):
                    left, mid, right = (
                        tf[3 * k + s, window, lane][7 + dy : 7 + dy + BLK, :] for s in range(3)
                    )
                    lo = jnp.where(same_x, mid, left)
                    hi = jnp.where(same_x, right, mid)
                    along.append(lo + fx * (hi - lo))
                lo = jnp.where(same_y, along[1], along[0])
                hi = jnp.where(same_y, along[2], along[1])
                across.append(lo + fy * (hi - lo))
            lo = jnp.where(lifted, across[1], across[0])
            hi = jnp.where(lifted, across[2], across[1])
            value = (lo + fz * (hi - lo)).astype(BF16)
            wb[here, lane] = value
            wf[pl.ds(pl.multiple_of(first + 8, 8), BLK), lane] = value.astype(F32)
        return carry

    def arrive(ch):
        for side, has, step in sides:
            @pl.when(has)
            def _():
                t_copy(1 - side, step, ch).wait_recv()
                f_copy(side, ch, core).start()

    def unpack(ch):
        for side, has, step in sides:
            @pl.when(has)
            def _():
                f_copy(side, ch, 1 - core).wait_recv()
        first, last = t_parts[ch]
        for which, slot in ((0, 0), (2, 1)):
            lax.fori_loop(
                first // BLK, last // BLK,
                spread(lambda r: near[slot, pl.ds(r, BLK), :], which), 0, unroll=6,
            )

    for load in loads[2:4]:
        load.wait()
    arrive(0)
    for side, edge, step in edges:
        @pl.when(edge)
        def _():
            i_copy(side, step).start()
    for ch, (first, last) in enumerate(w_parts):
        if ch < len(t_parts):
            unpack(ch)
        if ch + 1 < len(t_parts):
            arrive(ch + 1)
        lax.fori_loop(first // BLK, last // BLK, warp_block, 0, unroll=2)
        for side, has, step in sides:
            @pl.when(sends(side, ch))
            def _():
                w_copy(side, step, ch).start()

    for load in loads[4:7]:
        load.wait()

    def flat_block(r, carry):
        first = pl.multiple_of(r * BLK, BLK)
        here = pl.ds(first, BLK)
        centre = wf[pl.ds(pl.multiple_of(first + 8, 8), BLK), :]
        rest = (image[here, :].astype(F32) - centre) * 0.5
        window = wf[pl.ds(first, BLK + 16), :]
        grad_y = window[9 : 9 + BLK, :] - window[7 : 7 + BLK, :]
        fb[1, here, :] = (rest * grad_y).astype(BF16)
        place = lax.broadcasted_iota(jnp.int32, (BLK, cols), 1)
        after = jnp.where(place == cols - 1, 0.0, pltpu.roll(centre, cols - 1, 1))
        before = jnp.where(place == 0, 0.0, pltpu.roll(centre, 1, 1))
        fb[2, here, :] = (rest * (after - before)).astype(BF16)
        return carry

    lax.fori_loop(0, rows // BLK, flat_block, 0, unroll=4)

    lane = lax.broadcasted_iota(jnp.int32, (KM, KM * KM), 1)
    own_j = lane // KM == lax.broadcasted_iota(jnp.int32, (KM, KM * KM), 0)

    def along_y(c, first, last):
        return lax.dot_general(
            yt[first:last, :], fb[c, first:last, :], (((0,), (0,)), ((), ())), preferred_element_type=F32
        )

    def analyse(at_rows, sums):
        high, low_part = halves(jnp.concatenate([both[0:32] + both[32:64] for both in sums]))
        wide = dot(high, xt[0]) + dot(low_part, xt[0]) + dot(high, xt[1])
        for n, first in enumerate(at_rows):
            even, odd = wide[32 * n : 32 * n + 16], wide[32 * n + 16 : 32 * n + 32]
            real = even[:, 0:256] + odd[:, 256:512]
            imag = odd[:, 0:256] - even[:, 256:512]
            for part, value in ((0, real), (1, imag)):
                line_sum = jnp.sum(jnp.where(own_j, value, 0.0), axis=0, keepdims=True)
                at_row = first + 2 * part
                msg[at_row : at_row + 1, :] = line_sum[:, 0:128]
                msg[at_row + 1 : at_row + 2, :] = line_sum[:, 128:256]

    msg[8:16, :] = jnp.zeros((8, 128), F32)
    loads[1].wait()
    for c in range(6):
        high, low_part = halves(start[c])
        lanes = slice(64 * (c // 3), 64 * (c // 3) + 64)
        msg[8 + c % 3 : 9 + c % 3, lanes] = high.astype(F32)
        msg[11 + c % 3 : 12 + c % 3, lanes] = low_part.astype(F32)
    analyse((0, 4), (along_y(1, 0, rows), along_y(2, 0, rows)))
    cb_early[spot] = msg[...].astype(BF16)
    start_all(first_early)

    def centred_of(buffer, q):
        values = [buffer[p * ZLO + q].astype(F32) for p in range(4)]
        mean = (values[0] + values[1] + values[2] + values[3]) * 0.25
        return buffer[phase * ZLO + q].astype(F32) - mean

    def deep_block(r, carry):
        first = pl.multiple_of(r * BLK, BLK)
        here = pl.ds(first, BLK)
        centre = wf[pl.ds(pl.multiple_of(first + 8, 8), BLK), :]
        rest = (image[here, :].astype(F32) - centre) * 0.5
        grad_z = nearw[1, here, :].astype(F32) - nearw[0, here, :].astype(F32)
        fb[0, here, :] = (rest * grad_z).astype(BF16)
        return carry

    def across_block(slot):
        def body(r, carry):
            first = pl.multiple_of(r * BLK, BLK)
            here = pl.ds(first, BLK)
            mine = wf[pl.ds(pl.multiple_of(first + 8, 8), BLK), :] * (-0.5 if slot else 0.5)
            rest = neari[here, :].astype(F32) - nearw[slot, here, :].astype(F32)
            fb[3, here, :] = (rest * mine).astype(BF16)
            return carry
        return body

    def deep(ch):
        first, last = w_parts[ch]
        for side, has, step in sides:
            @pl.when(receives(side, ch))
            def _():
                w_copy(1 - side, step, ch).wait_recv()
        lax.fori_loop(first // BLK, last // BLK, deep_block, 0, unroll=True)

        slot = 0 if in_first(ch) else 1

        @pl.when(edge_down if in_first(ch) else edge_up)
        def _():
            lax.fori_loop(first // BLK, last // BLK, across_block(slot), 0, unroll=True)

        part = along_y(0, first, last)
        if ch == 0:
            acc[...] = part
        else:
            acc[...] += part

    for side, edge, step in edges:
        @pl.when(edge)
        def _():
            i_copy(1 - side, step).wait_recv()
    for ch in range(EARLY_AT):
        deep(ch)
    every["first_early"].wait_recv()
    for q in range(ZLO):
        value = centred_of(cb_early, q)
        high, low_part = halves(value[8:11] + value[11:14])
        msg[0:8, :] = value[0:8]
        msg[8:11, :] = high.astype(F32)
        msg[11:14, :] = low_part.astype(F32)
        db_early[column, 16 * q : 16 * q + 16, :] = msg[...].astype(BF16)
    start_all(second_early)
    for ch in range(EARLY_AT, len(w_parts)):
        deep(ch)
    start_row = pl.multiple_of(jnp.where(edge_up, middle, 0), 16)
    beyond = lax.dot_general(
        yt[pl.ds(start_row, middle), :], fb[3, pl.ds(start_row, middle), :],
        (((0,), (0,)), ((), ())), preferred_element_type=F32,
    )
    analyse((0, 4), (acc[...], beyond))

    cb[spot] = msg[...].astype(BF16)
    start_all(first_plane)
    for side, has, step in sides:
        @pl.when(has)
        def _():
            for ch in range(len(t_parts)):
                t_copy(side, step, ch).wait_send()
                f_copy(side, ch, core).wait_send()
        for ch in range(len(w_parts)):
            @pl.when(sends(side, ch))
            def _():
                w_copy(side, step, ch).wait_send()
    for side, edge, step in edges:
        @pl.when(edge)
        def _():
            i_copy(side, step).wait_send()
    for load in loads[7:]:
        load.wait()
    chosen = (lax.broadcasted_iota(jnp.int32, (slabs, 256), 0) == slab).astype(F32)
    zwave = jnp.dot(zfine[...], chosen, precision=HIGH, preferred_element_type=F32)
    zcos, zsin = zwave[0:KM], zwave[KM : 2 * KM]
    every["first_plane"].wait_recv()
    db[column] = jnp.concatenate([centred_of(cb, q)[0:8] for q in range(ZLO)]).astype(BF16)
    start_all(second_plane)
    every["second_early"].wait_recv()
    stacked = jnp.concatenate([db_early[x] for x in range(columns)])
    out_early = dot(early[0], stacked) + dot(early[1], stacked)
    wide = lax.dot_general(stacked, sel[...], (((0,), (0,)), ((), ())), preferred_element_type=F32)
    starts = []
    for c in range(6):
        lanes = slice(256 * (c % 3), 256 * (c % 3) + 256)
        total = jnp.zeros((KM, KM * KM), F32)
        for q in range(4):
            first = 64 * (c // 3) + KM * q
            total = jnp.where(lane % 4 == q, wide[first : first + KM, lanes], total)
        starts.append(total)
    every["second_plane"].wait_recv()
    m = KM
    inertia = jnp.concatenate([grid[0:m, :]] * 3)
    kernel = 1.0 / inertia
    wave_y = grid[m : m + 1, :]
    wave_x = grid[m + 1 : m + 2, :]
    stacked = jnp.concatenate([db[x] for x in range(columns)])
    out = dot(late[0], stacked) + dot(late[1], stacked)

    def modes_of(part):
        sides_of = [
            jnp.concatenate([
                out[32 * half + 16 * part : 32 * half + 16 * part + 16],
                out_early[64 * half + 32 * part : 64 * half + 32 * part + 32],
            ])
            for half in range(2)
        ]
        return jnp.concatenate(sides_of, axis=1)

    real, imag = modes_of(0), modes_of(1)
    vel_re = 0.5 * jnp.concatenate(starts[0:3]) + step_size * kernel * real
    vel_im = 0.5 * jnp.concatenate(starts[3:6]) + step_size * kernel * imag

    lane = lax.broadcasted_iota(jnp.int32, (m * m, 128), 1)
    mode = lax.broadcasted_iota(jnp.int32, (m * m, 128), 0)
    pick = (mode == 4 * slab + lane // m).astype(F32)
    taken = jnp.dot(
        jnp.concatenate([vel_re, vel_im]), pick, precision=HIGH, preferred_element_type=F32
    )
    diagonal = (
        lax.broadcasted_iota(jnp.int32, (m, 128), 1) % m
        == lax.broadcasted_iota(jnp.int32, (m, 128), 0)
    )
    for c in range(6):
        line = jnp.sum(jnp.where(diagonal, taken[c * m : c * m + m], 0.0), axis=0, keepdims=True)
        centred[c] = line[:, 0 : 4 * m]

    for step in range(STEPS):
        inputs_re = jnp.concatenate([vel_re, inertia * vel_re, wave_y * vel_re, wave_x * vel_re])
        inputs_im = jnp.concatenate([vel_im, inertia * vel_im, wave_y * vel_im, wave_x * vel_im])
        inputs = jnp.concatenate([inputs_re, inputs_im], axis=1).astype(BF16)
        flat = dot(inputs, forth[...])
        tall = jnp.concatenate([flat[:, 0:256], flat[:, 256:512]]).astype(BF16)
        fields = dot(up[...], tall)

        def field(kind, c):
            return fields[kind * 48 + c * m : kind * 48 + c * m + m]

        speed = [field(0, c) for c in range(3)]
        momentum = [field(1, c) for c in range(3)]
        advect = [
            field(2 + i, 0) * momentum[0] + field(2 + i, 1) * momentum[1] + field(2 + i, 2) * momentum[2]
            for i in range(3)
        ]
        outer = [momentum[i] * speed[j] for j in range(3) for i in range(3)]
        products = jnp.concatenate(advect + outer).astype(BF16)
        half = dot(down[...], products)
        wide = jnp.concatenate([half[0:144], half[144:288]], axis=1).astype(BF16)
        spec = dot(wide, back[...])
        coad_re = spec[0:48, 0:256] - wave_y * spec[48:96, 256:512] - wave_x * spec[96:144, 256:512]
        coad_im = spec[0:48, 256:512] + wave_y * spec[48:96, 0:256] + wave_x * spec[96:144, 0:256]
        vel_re = vel_re - time_step * kernel * coad_re
        vel_im = vel_im - time_step * kernel * coad_im

    rows_re, rows_im = [], []
    for c in range(3):
        re, im = vel_re[c * m : c * m + m], vel_im[c * m : c * m + m]
        plane_re = jnp.sum(re * zcos - im * zsin, axis=0, keepdims=True)
        plane_im = jnp.sum(re * zsin + im * zcos, axis=0, keepdims=True)
        rows_re.append(jnp.where(own_j, plane_re, 0.0))
        rows_im.append(jnp.where(own_j, plane_im, 0.0))
    high, low_part = halves(jnp.concatenate(rows_re + rows_im))
    wide = dot(high, xs[0]) + dot(low_part, xs[0]) + dot(high, xs[1])
    x_re = wide[0:48, 0:cols] - wide[48:96, cols:]
    x_im = wide[0:48, cols:] + wide[48:96, 0:cols]
    for c in range(3):
        pair = jnp.concatenate([x_re[c * m : c * m + m], x_im[c * m : c * m + m]])
        high, low_part = halves(pair)
        pairs[c] = jnp.concatenate([high, low_part, high])

    for copies in every.values():
        copies.wait_send()


def synth_kernel(pairs_hbm, modes_hbm, ys_hbm, centred_hbm, velocity_hbm, pairs, ys, velocity, in_sem, out_sem):
    loads = [
        pltpu.make_async_copy(ys_hbm, ys, in_sem.at[0]),
        *(pltpu.make_async_copy(pairs_hbm.at[c], pairs.at[c], in_sem.at[1 + c]) for c in range(3)),
    ]
    through = pltpu.make_async_copy(modes_hbm, centred_hbm, out_sem.at[3])
    for load in loads:
        load.start()
    through.start()
    copies = [
        pltpu.make_async_copy(velocity.at[c], velocity_hbm.at[c], out_sem.at[c]) for c in range(3)
    ]
    loads[0].wait()
    for c in range(3):
        loads[1 + c].wait()
        velocity[c] = dot(ys[...], pairs[c]).astype(BF16)
        copies[c].start()
    for copy in copies:
        copy.wait()
    through.wait()


def flash_call(tmpl, image, corner, frac, start, slabs):
    rows, cols = tmpl.shape
    tables = [jnp.asarray(t) for t in analysis_tables(rows, cols) + shooting_tables(slabs, rows, cols)]
    inputs = [tmpl, image, corner, frac, start] + tables[:-1]
    columns = slabs // ZLO
    dma = pltpu.SemaphoreType.DMA
    any_space = pl.BlockSpec(memory_space=pl.ANY)
    return pl.pallas_call(
        flash_kernel,
        out_shape=(
            jax.ShapeDtypeStruct((6, 1, 4 * KM), F32),
            jax.ShapeDtypeStruct((3, 6 * KM, cols), BF16),
        ),
        in_specs=[any_space] * len(inputs),
        out_specs=(pl.BlockSpec(memory_space=VMEM),) * 2,
        scratch_shapes=[VMEM(x.shape, x.dtype) for x in inputs] + [
            VMEM((2, rows, cols), BF16),
            VMEM((9, rows + 16, cols), F32),
            VMEM((rows + 16, cols), F32),
            VMEM((rows, cols), BF16),
            VMEM((2, rows, cols), BF16),
            VMEM((rows, cols), BF16),
            VMEM((4, rows, cols), BF16),
            VMEM((4 * KM, cols), F32),
            VMEM((16, 128), F32),
            VMEM((16, 16, 128), BF16),
            VMEM((columns, 32, 128), BF16),
            VMEM((16, 16, 128), BF16),
            VMEM((columns, 64, 128), BF16),
            dma((len(inputs),)),
            dma((2, len(T_ENDS))), dma((2, len(T_ENDS))), dma((2, len(T_ENDS))), dma((2, len(T_ENDS))),
            dma((2, len(W_ENDS))), dma((2, len(W_ENDS))), dma((1,)), dma((1,)),
            dma((1,)), dma((1,)), dma((1,)), dma((1,)),
            dma((1,)), dma((1,)), dma((1,)), dma((1,)),
        ],
        compiler_params=pltpu.CompilerParams(
            collective_id=0, has_side_effects=True, vmem_limit_bytes=54 * 2**20
        ),
        name="flash",
    )(*inputs), tables[-1]


def synth_call(pairs, modes, ys):
    rows, cols = ys.shape[0], pairs.shape[2]
    anywhere = pl.BlockSpec(memory_space=pl.ANY)
    return pl.pallas_call(
        synth_kernel,
        out_shape=(
            jax.ShapeDtypeStruct(modes.shape, F32),
            jax.ShapeDtypeStruct((3, rows, cols), BF16),
        ),
        in_specs=[anywhere] * 3,
        out_specs=(anywhere, anywhere),
        scratch_shapes=[
            VMEM(pairs.shape, BF16), VMEM(ys.shape, BF16), VMEM((3, rows, cols), BF16),
            pltpu.SemaphoreType.DMA((4,)), pltpu.SemaphoreType.DMA((4,)),
        ],
        compiler_params=pltpu.CompilerParams(vmem_limit_bytes=54 * 2**20),
        name="synth",
    )(pairs, modes, ys)


def local(template, phase_images, corner, fractions, start_modes):
    slabs = lax.axis_size("slab")
    start = jnp.transpose(start_modes, (1, 0, 2))
    (modes, pairs), ys = flash_call(
        template[0], phase_images[0, 0], corner[0, 0], fractions[0, :, 0], start, slabs
    )
    centred, velocity = synth_call(pairs, modes, ys)
    return (jnp.transpose(centred, (1, 0, 2)), velocity[None, :, None])


def solution(mesh):
    placed = (
        P("slab", None, None),
        P("phase", "slab", None, None),
        P("phase", "slab", None, None),
        P("phase", None, "slab", None, None),
        P("phase", None, "slab"),
    )
    return jax.shard_map(
        local,
        mesh=mesh,
        in_specs=placed,
        out_specs=(P("phase", None, "slab"), P("phase", None, "slab", None, None)),
        check_vma=False,
    )
```

```python
import functools
import math

import ml_dtypes
import numpy as np

import jax
import jax.numpy as jnp
from jax import lax
from jax.experimental import pallas as pl
from jax.experimental.pallas import tpu as pltpu
from jax.sharding import PartitionSpec as P

KM = 16
STEPS = 2
ZLO = 4
T_ENDS = (96, 224, 320, 384)
W_ENDS = (64, 192, 304, 352, 384)
BLK = 16
EARLY_AT = 3
HIGH = lax.Precision.HIGHEST
MESH = pl.DeviceIdType.MESH
step_size = 0.5
alpha_reg = 0.002
time_step = 0.025
F32 = jnp.float32
BF16 = jnp.bfloat16
VMEM = pltpu.VMEM


def wave(count, length, modes):
    places = np.arange(count, dtype=np.int64)
    freq = np.arange(modes, dtype=np.int64) - modes // 2
    angle = np.mod(places[:, None] * freq[None, :], length) * (2.0 * math.pi / length)
    return np.cos(angle), np.sin(angle)


def split(table):
    table = np.asarray(table, np.float32)
    high = table.astype(ml_dtypes.bfloat16)
    low = (table - high.astype(np.float32)).astype(ml_dtypes.bfloat16)
    return high, low


def halves(value):
    high = value.astype(BF16)
    low = (value - high.astype(F32)).astype(BF16)
    return high, low


def dot(left, right):
    return jnp.dot(left, right, preferred_element_type=F32)


def analysis_tables(rows, cols):
    ycos, ysin = wave(rows, rows, KM)
    xcos, xsin = wave(cols, cols, KM)
    yt = np.concatenate(split(np.concatenate([ycos, -ysin], axis=1)), axis=1)
    spread = np.concatenate([np.tile(xcos, (1, KM)), np.tile(xsin, (1, KM))], axis=1)
    xt = np.stack(split(spread))
    return yt, xt


def shooting_tables(slabs, rows, cols):
    m = KM
    zcos, zsin = wave(slabs, slabs, m)
    scale = 1.0 / math.sqrt(rows * cols * slabs)
    lifts = []
    for comps, lines in ((1, 8), (2, 16)):
        lift = np.zeros((2, 2, comps, m, slabs, lines))
        for half in range(2):
            for comp in range(comps):
                real, imag = comp * 4 + half, comp * 4 + 2 + half
                lift[half, 0, comp, :, :, real] = zcos.T * scale
                lift[half, 0, comp, :, :, imag] = zsin.T * scale
                lift[half, 1, comp, :, :, imag] = zcos.T * scale
                lift[half, 1, comp, :, :, real] = -zsin.T * scale
        if comps == 1:
            for s in range(slabs):
                across = s - 1 if s % ZLO == 0 else s + 1
                if s % ZLO in (0, ZLO - 1) and 0 <= across < slabs:
                    lift[..., s, 4:8] = lift[..., across, 0:4]
        lifts.append(np.concatenate(split(lift.reshape(4 * comps * m, slabs * lines))))
    late, early = lifts
    sel = np.zeros((slabs, 16, 3, slabs, 4), ml_dtypes.bfloat16)
    for row in range(3):
        for s in range(slabs):
            sel[s, 8 + row, row, s, :] = 1
            sel[s, 11 + row, row, s, :] = 1
    sel = sel.reshape(slabs * 16, 12 * slabs)
    gcos, gsin = wave(m, m, m)
    angle = np.arctan2(gsin, gcos)
    both = angle[:, None, :, None] + angle[None, :, None, :]
    cos2 = np.cos(both).reshape(m * m, m * m).T
    sin2 = np.sin(both).reshape(m * m, m * m).T
    forth = np.block([[cos2, sin2], [-sin2, cos2]]).astype(ml_dtypes.bfloat16)
    back = np.block([[cos2.T, -sin2.T], [sin2.T, cos2.T]]).astype(ml_dtypes.bfloat16)
    norm = float(m) ** (-1.5)
    freq = (np.arange(m) - m // 2) * (2.0 * math.pi / m)
    up = np.zeros((5, 3, m, 2, 4, 3, m))
    down = np.zeros((2, 3, 3, m, 4, 3, m))
    for c in range(3):
        up[0, c, :, 0, 0, c, :] = gcos * norm
        up[0, c, :, 1, 0, c, :] = -gsin * norm
        up[1, c, :, 0, 1, c, :] = gcos * norm
        up[1, c, :, 1, 1, c, :] = -gsin * norm
        up[2, c, :, 0, 0, c, :] = -gsin * norm * freq[None, :]
        up[2, c, :, 1, 0, c, :] = -gcos * norm * freq[None, :]
        for s in (2, 3):
            up[1 + s, c, :, 0, s, c, :] = -gsin * norm
            up[1 + s, c, :, 1, s, c, :] = -gcos * norm
        down[0, 0, c, :, 0, c, :] = gcos.T * norm
        down[1, 0, c, :, 0, c, :] = -gsin.T * norm
        down[0, 0, c, :, 1, c, :] = gsin.T * norm * freq[:, None]
        down[1, 0, c, :, 1, c, :] = gcos.T * norm * freq[:, None]
        for s in (1, 2):
            down[0, s, c, :, 1 + s, c, :] = gcos.T * norm
            down[1, s, c, :, 1 + s, c, :] = -gsin.T * norm
    up = up.reshape(15 * m, 24 * m).astype(ml_dtypes.bfloat16)
    down = down.reshape(18 * m, 12 * m).astype(ml_dtypes.bfloat16)
    whole = np.arange(m) - m // 2
    lanes_j, lanes_k = np.repeat(whole, m), np.tile(whole, m)
    squares = whole[:, None] ** 2 + (lanes_j**2 + lanes_k**2)[None, :]
    inertia = (1.0 + alpha_reg * squares) ** 2
    waves = np.stack([np.repeat(freq, m), np.tile(freq, m)])
    waves = np.concatenate([waves, np.zeros((6, m * m))])
    grid = np.concatenate([inertia, waves]).astype(np.float32)
    zfine = (np.concatenate([zcos.T, zsin.T]) * norm).astype(np.float32)
    ycos, ysin = wave(rows, rows, m)
    xcos, xsin = wave(cols, cols, m)
    spread = np.concatenate([np.tile(xcos.T, (m, 1)), np.tile(xsin.T, (m, 1))], axis=1)
    xs = np.stack(split(spread))
    yh, yl = split(np.concatenate([ycos, -ysin], axis=1))
    ys = np.concatenate([yh, yh, yl], axis=1)
    return sel, late, early, forth, back, up, down, grid, zfine, xs, ys


def flash_kernel(
    tmpl_hbm, image_hbm, corner_hbm, frac_hbm, start_hbm, yt_hbm, xt_hbm, sel_hbm, late_hbm, early_hbm, forth_hbm, back_hbm,
    up_hbm, down_hbm, grid_hbm, zfine_hbm, xs_hbm,
    centred, pairs,
    tmpl, image, corner, frac, start, yt, xt, sel, late, early, forth, back, up, down, grid, zfine, xs,
    near, tf, wf, wb, nearw, neari, fb, acc, msg, cb, db, cb_early, db_early,
    load_sem, t_send, t_recv, f_send, f_recv, w_send, w_recv, i_send, i_recv, c_send, c_recv,
    d_send, d_recv, ce_send, ce_recv, de_send, de_recv,
):
    rows, cols = tmpl.shape
    t_parts = [(a * rows // 384, b * rows // 384) for a, b in zip((0,) + T_ENDS, T_ENDS)]
    w_parts = [(a * rows // 384, b * rows // 384) for a, b in zip((0,) + W_ENDS, W_ENDS)]
    phase = lax.axis_index("phase")
    slab = lax.axis_index("slab")
    slabs = lax.axis_size("slab")
    columns = slabs // ZLO
    low = slab % ZLO
    column = slab // ZLO
    spot = phase * ZLO + low
    has_down, has_up = slab > 0, slab < slabs - 1
    edge_down = jnp.logical_and(has_down, low == 0)
    edge_up = jnp.logical_and(has_up, low == ZLO - 1)
    other = (phase + 2) % 4
    core = phase % 2
    sibling = phase + 1 - 2 * core
    t_phase = (jnp.where(edge_down, other, phase), jnp.where(edge_up, other, phase))

    def at(p, s):
        return {"phase": p, "slab": s}

    def mate(d):
        there = (spot + d) % 16
        return at(there // ZLO, slab - low + there % ZLO)

    def peer(d):
        return at(phase, ((column + d) % columns) * ZLO + low)

    barrier = pltpu.get_barrier_semaphore()

    def greet(d, carry):
        pl.semaphore_signal(barrier, inc=1, device_id=mate(d), device_id_type=MESH)
        pl.semaphore_signal(barrier, inc=1, device_id=peer(d), device_id_type=MESH)
        return carry

    for edge, step in ((edge_down, -1), (edge_up, 1)):
        @pl.when(edge)
        def _():
            pl.semaphore_signal(barrier, inc=1, device_id=at(phase, slab + step), device_id_type=MESH)
            pl.semaphore_signal(barrier, inc=1, device_id=at(other, slab + step), device_id_type=MESH)

    greet(1, 0)
    greet(15, 0)
    lax.fori_loop(2, 15, greet, 0)

    loads = [
        pltpu.make_async_copy(source, target, load_sem.at[i])
        for i, (source, target) in enumerate((
            (tmpl_hbm, tmpl), (start_hbm, start), (corner_hbm, corner), (frac_hbm, frac), (image_hbm, image),
            (yt_hbm, yt), (xt_hbm, xt), (sel_hbm, sel), (late_hbm, late), (early_hbm, early), (forth_hbm, forth), (back_hbm, back),
            (up_hbm, up), (down_hbm, down), (grid_hbm, grid), (zfine_hbm, zfine), (xs_hbm, xs),
        ))
    ]
    for load in loads:
        load.start()

    pl.semaphore_wait(
        barrier, 30 + 2 * edge_down.astype(jnp.int32) + 2 * edge_up.astype(jnp.int32)
    )

    sides = ((0, has_down, -1), (1, has_up, 1))

    def t_rows(ch, which):
        first, last = t_parts[ch]
        size = (last - first) // 2
        return pl.ds(pl.multiple_of(first + which * size, 16), size)

    def t_copy(side, step, ch):
        part = t_rows(ch, core)
        return pltpu.make_async_remote_copy(
            src_ref=tmpl_hbm.at[part], dst_ref=near.at[1 - side, part],
            send_sem=t_send.at[side, ch], recv_sem=t_recv.at[1 - side, ch],
            device_id=at(t_phase[side], slab + step), device_id_type=MESH,
        )

    def f_copy(slot, ch, which):
        part = t_rows(ch, which)
        return pltpu.make_async_remote_copy(
            src_ref=near.at[slot, part], dst_ref=near.at[slot, part],
            send_sem=f_send.at[slot, ch], recv_sem=f_recv.at[slot, ch],
            device_id=at(sibling, slab), device_id_type=MESH,
        )

    def w_copy(side, step, ch):
        first, last = w_parts[ch]
        part = pl.ds(first, last - first)
        return pltpu.make_async_remote_copy(
            src_ref=wb.at[part], dst_ref=nearw.at[1 - side, part],
            send_sem=w_send.at[side, ch], recv_sem=w_recv.at[1 - side, ch],
            device_id=at(phase, slab + step), device_id_type=MESH,
        )

    def in_first(ch):
        return w_parts[ch][1] <= rows // 2

    def sends(side, ch):
        if side:
            return has_up if in_first(ch) else jnp.logical_and(has_up, low != ZLO - 1)
        return jnp.logical_and(has_down, low != 0) if in_first(ch) else has_down

    def receives(slot, ch):
        if slot:
            return jnp.logical_and(has_up, low != ZLO - 1) if in_first(ch) else has_up
        return has_down if in_first(ch) else jnp.logical_and(has_down, low != 0)

    def i_copy(side, step):
        part = pl.ds(0 if side else rows // 2, rows // 2)
        return pltpu.make_async_remote_copy(
            src_ref=image_hbm.at[part], dst_ref=neari.at[part],
            send_sem=i_send.at[0], recv_sem=i_recv.at[0],
            device_id=at(phase, slab + step), device_id_type=MESH,
        )

    for ch in range(len(t_parts)):
        for side, has, step in sides:
            @pl.when(has)
            def _():
                t_copy(side, step, ch).start()

    edges = ((0, edge_down, -1), (1, edge_up, 1))

    def spread(source, which):
        def body(r, carry):
            first = pl.multiple_of(r * BLK, BLK)
            value = source(first).astype(F32)
            there = pl.ds(pl.multiple_of(first + 8, 8), BLK)
            tf[3 * which, there, :] = pltpu.roll(value, 1, 1)
            tf[3 * which + 1, there, :] = value
            tf[3 * which + 2, there, :] = pltpu.roll(value, cols - 1, 1)
            return carry
        return body

    loads[0].wait()
    lax.fori_loop(0, rows // BLK, spread(lambda r: tmpl[pl.ds(r, BLK), :], 1), 0, unroll=6)
    edge_rows = jnp.zeros((8, cols), F32)
    for k in range(9):
        tf[k, 0:8, :] = edge_rows
        tf[k, rows + 8 : rows + 16, :] = edge_rows
    wf[0:8, :] = edge_rows
    wf[rows + 8 : rows + 16, :] = edge_rows
    middle = rows // 2
    is_edge = jnp.logical_or(edge_down, edge_up)

    @pl.when(jnp.logical_not(has_down))
    def _():
        near[0] = jnp.zeros((rows, cols), BF16)
        nearw[0] = jnp.zeros((rows, cols), BF16)

    @pl.when(jnp.logical_not(has_up))
    def _():
        near[1] = jnp.zeros((rows, cols), BF16)
        nearw[1] = jnp.zeros((rows, cols), BF16)

    @pl.when(edge_down)
    def _():
        nearw[0, middle:rows, :] = jnp.zeros((middle, cols), BF16)

    @pl.when(edge_up)
    def _():
        nearw[1, 0:middle, :] = jnp.zeros((middle, cols), BF16)

    @pl.when(jnp.logical_not(is_edge))
    def _():
        fb[3] = jnp.zeros((rows, cols), BF16)

    def first_plane(d):
        return pltpu.make_async_remote_copy(
            src_ref=cb.at[spot], dst_ref=cb.at[spot],
            send_sem=c_send.at[0], recv_sem=c_recv.at[0],
            device_id=mate(d), device_id_type=MESH,
        )

    def second_plane(d):
        return pltpu.make_async_remote_copy(
            src_ref=db.at[column], dst_ref=db.at[column],
            send_sem=d_send.at[0], recv_sem=d_recv.at[0],
            device_id=peer(d), device_id_type=MESH,
        )

    def first_early(d):
        return pltpu.make_async_remote_copy(
            src_ref=cb_early.at[spot], dst_ref=cb_early.at[spot],
            send_sem=ce_send.at[0], recv_sem=ce_recv.at[0],
            device_id=mate(d), device_id_type=MESH,
        )

    def second_early(d):
        return pltpu.make_async_remote_copy(
            src_ref=db_early.at[column], dst_ref=db_early.at[column],
            send_sem=de_send.at[0], recv_sem=de_recv.at[0],
            device_id=peer(d), device_id_type=MESH,
        )

    def start_all(copy):
        def body(d, carry):
            copy(d).start()
            return carry
        lax.fori_loop(1, 16, body, 0)

    def all_of(buffer, send, recv):
        part = buffer.at[pl.ds(0, 15)]
        return pltpu.make_async_remote_copy(
            src_ref=part, dst_ref=part, send_sem=send.at[0], recv_sem=recv.at[0],
            device_id=mate(1), device_id_type=MESH,
        )

    every = {
        "first_plane": all_of(cb, c_send, c_recv),
        "second_plane": all_of(db, d_send, d_recv),
        "first_early": all_of(cb_early, ce_send, ce_recv), "second_early": all_of(db_early, de_send, de_recv),
    }


    col = lax.broadcasted_iota(jnp.int32, (BLK, 128), 1)
    line = lax.broadcasted_iota(jnp.int32, (BLK, 128), 0)

    def warp_block(r, carry):
        first = pl.multiple_of(r * BLK, BLK)
        here = pl.ds(first, BLK)
        window = pl.ds(first, BLK + 16)
        for lt in range(cols // 128):
            lane = slice(lt * 128, lt * 128 + 128)
            code = corner[here, lane]
            fz = frac[0, here, lane].astype(F32)
            fy = frac[1, here, lane].astype(F32)
            fx = frac[2, here, lane].astype(F32)
            lifted = code >= 4
            ybit = jnp.where(line + first == 0, 2, jnp.where(line + first == rows - 1, 0, code & 2))
            same_y = ybit == 2
            xbit = code & 1
            if lt == 0:
                xbit = jnp.where(col == 0, 1, xbit)
            if lt == cols // 128 - 1:
                xbit = jnp.where(col == 127, 0, xbit)
            same_x = xbit == 1
            across = []
            for k in range(3):
                along = []
                for dy in range(3):
                    left, mid, right = (
                        tf[3 * k + s, window, lane][7 + dy : 7 + dy + BLK, :] for s in range(3)
                    )
                    lo = jnp.where(same_x, mid, left)
                    hi = jnp.where(same_x, right, mid)
                    along.append(lo + fx * (hi - lo))
                lo = jnp.where(same_y, along[1], along[0])
                hi = jnp.where(same_y, along[2], along[1])
                across.append(lo + fy * (hi - lo))
            lo = jnp.where(lifted, across[1], across[0])
            hi = jnp.where(lifted, across[2], across[1])
            value = (lo + fz * (hi - lo)).astype(BF16)
            wb[here, lane] = value
            wf[pl.ds(pl.multiple_of(first + 8, 8), BLK), lane] = value.astype(F32)
        return carry

    def arrive(ch):
        for side, has, step in sides:
            @pl.when(has)
            def _():
                t_copy(1 - side, step, ch).wait_recv()
                f_copy(side, ch, core).start()

    def unpack(ch):
        for side, has, step in sides:
            @pl.when(has)
            def _():
                f_copy(side, ch, 1 - core).wait_recv()
        first, last = t_parts[ch]
        for which, slot in ((0, 0), (2, 1)):
            lax.fori_loop(
                first // BLK, last // BLK,
                spread(lambda r: near[slot, pl.ds(r, BLK), :], which), 0, unroll=6,
            )

    for load in loads[2:4]:
        load.wait()
    arrive(0)
    for side, edge, step in edges:
        @pl.when(edge)
        def _():
            i_copy(side, step).start()
    for ch, (first, last) in enumerate(w_parts):
        if ch < len(t_parts):
            unpack(ch)
        if ch + 1 < len(t_parts):
            arrive(ch + 1)
        lax.fori_loop(first // BLK, last // BLK, warp_block, 0, unroll=2)
        for side, has, step in sides:
            @pl.when(sends(side, ch))
            def _():
                w_copy(side, step, ch).start()

    for load in loads[4:7]:
        load.wait()

    def flat_block(r, carry):
        first = pl.multiple_of(r * BLK, BLK)
        here = pl.ds(first, BLK)
        centre = wf[pl.ds(pl.multiple_of(first + 8, 8), BLK), :]
        rest = (image[here, :].astype(F32) - centre) * 0.5
        window = wf[pl.ds(first, BLK + 16), :]
        grad_y = window[9 : 9 + BLK, :] - window[7 : 7 + BLK, :]
        fb[1, here, :] = (rest * grad_y).astype(BF16)
        place = lax.broadcasted_iota(jnp.int32, (BLK, cols), 1)
        after = jnp.where(place == cols - 1, 0.0, pltpu.roll(centre, cols - 1, 1))
        before = jnp.where(place == 0, 0.0, pltpu.roll(centre, 1, 1))
        fb[2, here, :] = (rest * (after - before)).astype(BF16)
        return carry

    lax.fori_loop(0, rows // BLK, flat_block, 0, unroll=4)

    lane = lax.broadcasted_iota(jnp.int32, (KM, KM * KM), 1)
    own_j = lane // KM == lax.broadcasted_iota(jnp.int32, (KM, KM * KM), 0)

    def along_y(c, first, last):
        return lax.dot_general(
            yt[first:last, :], fb[c, first:last, :], (((0,), (0,)), ((), ())), preferred_element_type=F32
        )

    def analyse(at_rows, sums):
        high, low_part = halves(jnp.concatenate([both[0:32] + both[32:64] for both in sums]))
        count = high.shape[0]
        wide = dot(jnp.concatenate([high, low_part]), xt[0])
        wide = wide[:count] + wide[count:] + dot(high, xt[1])
        for n, first in enumerate(at_rows):
            even, odd = wide[32 * n : 32 * n + 16], wide[32 * n + 16 : 32 * n + 32]
            real = even[:, 0:256] + odd[:, 256:512]
            imag = odd[:, 0:256] - even[:, 256:512]
            for part, value in ((0, real), (1, imag)):
                line_sum = jnp.sum(jnp.where(own_j, value, 0.0), axis=0, keepdims=True)
                at_row = first + 2 * part
                msg[at_row : at_row + 1, :] = line_sum[:, 0:128]
                msg[at_row + 1 : at_row + 2, :] = line_sum[:, 128:256]

    msg[8:16, :] = jnp.zeros((8, 128), F32)
    loads[1].wait()
    for c in range(6):
        high, low_part = halves(start[c])
        lanes = slice(64 * (c // 3), 64 * (c // 3) + 64)
        msg[8 + c % 3 : 9 + c % 3, lanes] = high.astype(F32)
        msg[11 + c % 3 : 12 + c % 3, lanes] = low_part.astype(F32)
    analyse((0, 4), (along_y(1, 0, rows), along_y(2, 0, rows)))
    cb_early[spot] = msg[...].astype(BF16)
    start_all(first_early)

    def centred_of(buffer, q):
        values = [buffer[p * ZLO + q].astype(F32) for p in range(4)]
        mean = (values[0] + values[1] + values[2] + values[3]) * 0.25
        return buffer[phase * ZLO + q].astype(F32) - mean

    def deep_block(r, carry):
        first = pl.multiple_of(r * BLK, BLK)
        here = pl.ds(first, BLK)
        centre = wf[pl.ds(pl.multiple_of(first + 8, 8), BLK), :]
        rest = (image[here, :].astype(F32) - centre) * 0.5
        grad_z = nearw[1, here, :].astype(F32) - nearw[0, here, :].astype(F32)
        fb[0, here, :] = (rest * grad_z).astype(BF16)
        return carry

    def across_block(slot):
        def body(r, carry):
            first = pl.multiple_of(r * BLK, BLK)
            here = pl.ds(first, BLK)
            mine = wf[pl.ds(pl.multiple_of(first + 8, 8), BLK), :] * (-0.5 if slot else 0.5)
            rest = neari[here, :].astype(F32) - nearw[slot, here, :].astype(F32)
            fb[3, here, :] = (rest * mine).astype(BF16)
            return carry
        return body

    def deep(ch):
        first, last = w_parts[ch]
        for side, has, step in sides:
            @pl.when(receives(side, ch))
            def _():
                w_copy(1 - side, step, ch).wait_recv()
        lax.fori_loop(first // BLK, last // BLK, deep_block, 0, unroll=True)

        slot = 0 if in_first(ch) else 1

        @pl.when(edge_down if in_first(ch) else edge_up)
        def _():
            lax.fori_loop(first // BLK, last // BLK, across_block(slot), 0, unroll=True)

        part = along_y(0, first, last)
        if ch == 0:
            acc[...] = part
        else:
            acc[...] += part

    for side, edge, step in edges:
        @pl.when(edge)
        def _():
            i_copy(1 - side, step).wait_recv()
    for ch in range(EARLY_AT):
        deep(ch)
    every["first_early"].wait_recv()
    for q in range(ZLO):
        value = centred_of(cb_early, q)
        high, low_part = halves(value[8:11] + value[11:14])
        msg[0:8, :] = value[0:8]
        msg[8:11, :] = high.astype(F32)
        msg[11:14, :] = low_part.astype(F32)
        db_early[column, 16 * q : 16 * q + 16, :] = msg[...].astype(BF16)
    start_all(second_early)
    for ch in range(EARLY_AT, len(w_parts)):
        deep(ch)
    start_row = pl.multiple_of(jnp.where(edge_up, middle, 0), 16)
    beyond = lax.dot_general(
        yt[pl.ds(start_row, middle), :], fb[3, pl.ds(start_row, middle), :],
        (((0,), (0,)), ((), ())), preferred_element_type=F32,
    )
    analyse((0, 4), (acc[...], beyond))

    cb[spot] = msg[...].astype(BF16)
    start_all(first_plane)
    for side, has, step in sides:
        @pl.when(has)
        def _():
            for ch in range(len(t_parts)):
                t_copy(side, step, ch).wait_send()
                f_copy(side, ch, core).wait_send()
        for ch in range(len(w_parts)):
            @pl.when(sends(side, ch))
            def _():
                w_copy(side, step, ch).wait_send()
    for side, edge, step in edges:
        @pl.when(edge)
        def _():
            i_copy(side, step).wait_send()
    for load in loads[7:]:
        load.wait()
    chosen = (lax.broadcasted_iota(jnp.int32, (slabs, 256), 0) == slab).astype(F32)
    zwave = jnp.dot(zfine[...], chosen, precision=HIGH, preferred_element_type=F32)
    zcos, zsin = zwave[0:KM], zwave[KM : 2 * KM]
    every["first_plane"].wait_recv()
    db[column] = jnp.concatenate([centred_of(cb, q)[0:8] for q in range(ZLO)]).astype(BF16)
    start_all(second_plane)
    every["second_early"].wait_recv()
    stacked = jnp.concatenate([db_early[x] for x in range(columns)])
    out_early = dot(early[...], stacked)
    out_early = out_early[0:128] + out_early[128:256]
    wide = lax.dot_general(stacked, sel[...], (((0,), (0,)), ((), ())), preferred_element_type=F32)
    starts = []
    for c in range(6):
        lanes = slice(256 * (c % 3), 256 * (c % 3) + 256)
        total = jnp.zeros((KM, KM * KM), F32)
        for q in range(4):
            first = 64 * (c // 3) + KM * q
            total = jnp.where(lane % 4 == q, wide[first : first + KM, lanes], total)
        starts.append(total)
    m = KM
    inertia = jnp.concatenate([grid[0:m, :]] * 3)
    kernel = 1.0 / inertia
    wave_y = grid[m : m + 1, :]
    wave_x = grid[m + 1 : m + 2, :]
    start_re = 0.5 * jnp.concatenate(starts[0:3])
    start_im = 0.5 * jnp.concatenate(starts[3:6])
    for name in ("first_plane", "first_early", "second_early"):
        every[name].wait_send()
    every["second_plane"].wait_recv()
    stacked = jnp.concatenate([db[x] for x in range(columns)])
    out = dot(late[...], stacked)
    out = out[0:64] + out[64:128]

    def modes_of(part):
        sides_of = [
            jnp.concatenate([
                out[32 * half + 16 * part : 32 * half + 16 * part + 16],
                out_early[64 * half + 32 * part : 64 * half + 32 * part + 32],
            ])
            for half in range(2)
        ]
        return jnp.concatenate(sides_of, axis=1)

    real, imag = modes_of(0), modes_of(1)
    vel_re = start_re + step_size * kernel * real
    vel_im = start_im + step_size * kernel * imag

    lane = lax.broadcasted_iota(jnp.int32, (m * m, 128), 1)
    mode = lax.broadcasted_iota(jnp.int32, (m * m, 128), 0)
    pick = (mode == 4 * slab + lane // m).astype(F32)
    taken = jnp.dot(
        jnp.concatenate([vel_re, vel_im]), pick, precision=HIGH, preferred_element_type=F32
    )
    diagonal = (
        lax.broadcasted_iota(jnp.int32, (m, 128), 1) % m
        == lax.broadcasted_iota(jnp.int32, (m, 128), 0)
    )
    for c in range(6):
        line = jnp.sum(jnp.where(diagonal, taken[c * m : c * m + m], 0.0), axis=0, keepdims=True)
        centred[c] = line[:, 0 : 4 * m]

    for step in range(STEPS):
        inputs_re = jnp.concatenate([vel_re, inertia * vel_re, wave_y * vel_re, wave_x * vel_re])
        inputs_im = jnp.concatenate([vel_im, inertia * vel_im, wave_y * vel_im, wave_x * vel_im])
        inputs = jnp.concatenate([inputs_re, inputs_im], axis=1).astype(BF16)
        flat = dot(inputs, forth[...])
        tall = jnp.concatenate([flat[:, 0:256], flat[:, 256:512]]).astype(BF16)
        fields = dot(up[...], tall)

        def field(kind, c):
            return fields[kind * 48 + c * m : kind * 48 + c * m + m]

        speed = [field(0, c) for c in range(3)]
        momentum = [field(1, c) for c in range(3)]
        advect = [
            field(2 + i, 0) * momentum[0] + field(2 + i, 1) * momentum[1] + field(2 + i, 2) * momentum[2]
            for i in range(3)
        ]
        outer = [momentum[i] * speed[j] for j in range(3) for i in range(3)]
        products = jnp.concatenate(advect + outer).astype(BF16)
        half = dot(down[...], products)
        wide = jnp.concatenate([half[0:144], half[144:288]], axis=1).astype(BF16)
        spec = dot(wide, back[...])
        coad_re = spec[0:48, 0:256] - wave_y * spec[48:96, 256:512] - wave_x * spec[96:144, 256:512]
        coad_im = spec[0:48, 256:512] + wave_y * spec[48:96, 0:256] + wave_x * spec[96:144, 0:256]
        vel_re = vel_re - time_step * kernel * coad_re
        vel_im = vel_im - time_step * kernel * coad_im

    rows_re, rows_im = [], []
    for c in range(3):
        re, im = vel_re[c * m : c * m + m], vel_im[c * m : c * m + m]
        plane_re = jnp.sum(re * zcos - im * zsin, axis=0, keepdims=True)
        plane_im = jnp.sum(re * zsin + im * zcos, axis=0, keepdims=True)
        rows_re.append(jnp.where(own_j, plane_re, 0.0))
        rows_im.append(jnp.where(own_j, plane_im, 0.0))
    high, low_part = halves(jnp.concatenate(rows_re + rows_im))
    wide = dot(jnp.concatenate([high, low_part]), xs[0])
    wide = wide[0:96] + wide[96:192] + dot(high, xs[1])
    x_re = wide[0:48, 0:cols] - wide[48:96, cols:]
    x_im = wide[0:48, cols:] + wide[48:96, 0:cols]
    for c in range(3):
        pair = jnp.concatenate([x_re[c * m : c * m + m], x_im[c * m : c * m + m]])
        high, low_part = halves(pair)
        pairs[c] = jnp.concatenate([high, low_part, high])

    every["second_plane"].wait_send()


def synth_kernel(pairs_hbm, modes_hbm, ys_hbm, centred_hbm, velocity_hbm, pairs, ys, velocity, in_sem, out_sem):
    loads = [
        pltpu.make_async_copy(ys_hbm, ys, in_sem.at[0]),
        *(pltpu.make_async_copy(pairs_hbm.at[c], pairs.at[c], in_sem.at[1 + c]) for c in range(3)),
    ]
    through = pltpu.make_async_copy(modes_hbm, centred_hbm, out_sem.at[3])
    for load in loads:
        load.start()
    through.start()
    copies = [
        pltpu.make_async_copy(velocity.at[c], velocity_hbm.at[c], out_sem.at[c]) for c in range(3)
    ]
    loads[0].wait()
    for c in range(3):
        loads[1 + c].wait()
        velocity[c] = dot(ys[...], pairs[c]).astype(BF16)
        copies[c].start()
    for copy in copies:
        copy.wait()
    through.wait()


def flash_call(tmpl, image, corner, frac, start, slabs):
    rows, cols = tmpl.shape
    tables = [jnp.asarray(t) for t in analysis_tables(rows, cols) + shooting_tables(slabs, rows, cols)]
    inputs = [tmpl, image, corner, frac, start] + tables[:-1]
    columns = slabs // ZLO
    dma = pltpu.SemaphoreType.DMA
    any_space = pl.BlockSpec(memory_space=pl.ANY)
    return pl.pallas_call(
        flash_kernel,
        out_shape=(
            jax.ShapeDtypeStruct((6, 1, 4 * KM), F32),
            jax.ShapeDtypeStruct((3, 6 * KM, cols), BF16),
        ),
        in_specs=[any_space] * len(inputs),
        out_specs=(pl.BlockSpec(memory_space=VMEM),) * 2,
        scratch_shapes=[VMEM(x.shape, x.dtype) for x in inputs] + [
            VMEM((2, rows, cols), BF16),
            VMEM((9, rows + 16, cols), F32),
            VMEM((rows + 16, cols), F32),
            VMEM((rows, cols), BF16),
            VMEM((2, rows, cols), BF16),
            VMEM((rows, cols), BF16),
            VMEM((4, rows, cols), BF16),
            VMEM((4 * KM, cols), F32),
            VMEM((16, 128), F32),
            VMEM((16, 16, 128), BF16),
            VMEM((columns, 32, 128), BF16),
            VMEM((16, 16, 128), BF16),
            VMEM((columns, 64, 128), BF16),
            dma((len(inputs),)),
            dma((2, len(T_ENDS))), dma((2, len(T_ENDS))), dma((2, len(T_ENDS))), dma((2, len(T_ENDS))),
            dma((2, len(W_ENDS))), dma((2, len(W_ENDS))), dma((1,)), dma((1,)),
            dma((1,)), dma((1,)), dma((1,)), dma((1,)),
            dma((1,)), dma((1,)), dma((1,)), dma((1,)),
        ],
        compiler_params=pltpu.CompilerParams(
            collective_id=0, has_side_effects=True, vmem_limit_bytes=54 * 2**20
        ),
        name="flash",
    )(*inputs), tables[-1]


def synth_call(pairs, modes, ys):
    rows, cols = ys.shape[0], pairs.shape[2]
    anywhere = pl.BlockSpec(memory_space=pl.ANY)
    return pl.pallas_call(
        synth_kernel,
        out_shape=(
            jax.ShapeDtypeStruct(modes.shape, F32),
            jax.ShapeDtypeStruct((3, rows, cols), BF16),
        ),
        in_specs=[anywhere] * 3,
        out_specs=(anywhere, anywhere),
        scratch_shapes=[
            VMEM(pairs.shape, BF16), VMEM(ys.shape, BF16), VMEM((3, rows, cols), BF16),
            pltpu.SemaphoreType.DMA((4,)), pltpu.SemaphoreType.DMA((4,)),
        ],
        compiler_params=pltpu.CompilerParams(vmem_limit_bytes=54 * 2**20),
        name="synth",
    )(pairs, modes, ys)


def local(template, phase_images, corner, fractions, start_modes):
    slabs = lax.axis_size("slab")
    start = jnp.transpose(start_modes, (1, 0, 2))
    (modes, pairs), ys = flash_call(
        template[0], phase_images[0, 0], corner[0, 0], fractions[0, :, 0], start, slabs
    )
    centred, velocity = synth_call(pairs, modes, ys)
    return (jnp.transpose(centred, (1, 0, 2)), velocity[None, :, None])


def solution(mesh):
    placed = (
        P("slab", None, None),
        P("phase", "slab", None, None),
        P("phase", "slab", None, None),
        P("phase", None, "slab", None, None),
        P("phase", None, "slab"),
    )
    return jax.shard_map(
        local,
        mesh=mesh,
        in_specs=placed,
        out_specs=(P("phase", None, "slab"), P("phase", None, "slab", None, None)),
        check_vma=False,
    )
```
